128 devices in a mesh: table: 64 (over z, y, x), ctx: 2 (over core).
Axes of the slice: x: 4, y: 4, z: 4, core: 2. Of those that a mesh axis runs over, the one named last changes fastest.
Arguments:
- item_table: float32 [131072, 256], P('table'), may hold values from -3 to 3
- serve_rows: int32 [4096, 128], P('table', 'ctx'), may hold values from 0 to 2047, as said below
- token_slots: int32 [64, 2048, 4], P('table', 'ctx'), may hold values from 0 to 4095
- lengths: int32 [64], P('table'), may hold values from 1 to 2048, as said below
- w_proj: bfloat16 [256, 2048], replicated, may hold values from -0.375 to 0.375
- w_out: bfloat16 [512, 256], replicated, may hold values from -0.25 to 0.25
- grad_out: bfloat16 [64, 2048, 256], P('table', 'ctx'), may hold values from -6 to 6
Outputs:
- layer_out: bfloat16 [64, 2048, 256], P('table', 'ctx')
- grad_table: float32 [131072, 256], P(('table', 'ctx'))
The draws below stay inside these ranges and needn't reach their ends.
Inputs may be any that keep to these rules, and one draw needn't show every extreme that they name: `serve_rows`: the 64 rows that one owner serves to one requesting device are distinct. `lengths`: some history has all 2048 actions.
All inputs are finite; a program needn't handle non-finite values.
Results may differ from the reference program's by a relative error of at most 0.009.
Values may be sent and summed in bfloat16 or wider, within the bound.
A program may use at most 192 MiB of HBM per device.

```python
import math
import jax
import jax.numpy as jnp
import numpy as np
from jax import lax

D = 256
HEADS = 4
HEAD = 128
FEATS = 4
TOK_DEV = 1024
ROWS_DEV = 2048
HD = 512
LEN = 2048
BATCH = 64
CAP = 64
SLOTS = 4096
SERVE = 4096
SERVE_COLS = 128
TABLE_ROWS = 131072


def draw_serve_rows(key, part):
    scores = jax.random.randint(key, (SERVE, SERVE_COLS // CAP, ROWS_DEV), 0, 2 ** 30)
    order = jnp.argsort(scores, axis=-1, stable=True)
    return order[..., :CAP].reshape(SERVE, SERVE_COLS).astype(jnp.int32)


def draw_lengths(key, part):
    first_key = jax.random.fold_in(key, 11)
    second_key = jax.random.fold_in(key, 23)
    drawn = jax.random.randint(first_key, (BATCH,), 1, LEN + 1)
    longest = jax.random.randint(second_key, (), 0, BATCH)
    return jnp.where(jnp.arange(BATCH) == longest, LEN, drawn).astype(jnp.int32)


def with_ends(entries, own_key, least, high):
    index_at = [jax.random.randint(jax.random.fold_in(own_key, axis), (), 0, length) for axis, length in enumerate(entries.shape)]
    main_axis = entries.shape.index(max(entries.shape))
    next_to = index_at[:main_axis] + [(index_at[main_axis] + 1) % entries.shape[main_axis]] + index_at[main_axis + 1:]
    return entries.at[tuple(index_at)].set(least).at[tuple(next_to)].set(high)


def block_levels(key, shape, shards, smallest, largest):
    level, own = 1.0, jax.random.fold_in(key, 6)
    for axis_at, parts in shards:
        steps = jnp.exp(jax.random.uniform(jax.random.fold_in(own, axis_at), (parts,), jnp.float32, smallest / len(shards), largest / len(shards)))
        level = level * jnp.repeat(steps, shape[axis_at] // parts).reshape([-1 if axis == axis_at else 1 for axis in range(len(shape))])
    return level


def cumulative_ranks(number_of, lean):
    loads = [(1 << 20) // math.isqrt(grade ** lean) + 1 for grade in range(1, number_of + 1)]
    spread = 1 + sum(loads) // (1 << 30)
    return np.cumsum(np.array([max(1, weight // spread) for weight in loads]))


def ranked_ids(own_key, shape, count, skew):
    listing = cumulative_ranks(count, skew)
    lot = jax.random.randint(jax.random.fold_in(own_key, 1), shape, 0, int(listing[count - 1]))
    grade = jnp.searchsorted(jnp.asarray(listing, jnp.int32), lot, side="right")
    return jax.random.permutation(jax.random.fold_in(own_key, 2), count)[grade].astype(jnp.int32)


def normal_values(own_key, dims, width, limit, shards=(), held_as=jnp.bfloat16):
    result = jax.random.normal(own_key, dims, jnp.float32) * width
    if len(shards) > 0:
        result = block_levels(own_key, dims, shards, -0.22, 0.18) * result
    return jnp.clip(result, min=-limit, max=limit).astype(held_as)


def setup_inputs(seed: int = 0) -> dict:
    key_of = jax.random.split(jax.random.key(seed), 8)
    item_table = normal_values(key_of[0], (TABLE_ROWS, D), 0.5, 3.0, ((0, 64),), jnp.float32)
    serve_rows = draw_serve_rows(jax.random.fold_in(key_of[7], 71), 0)
    token_slots = with_ends(ranked_ids(key_of[2], (BATCH, LEN, FEATS), SLOTS, 1), jax.random.fold_in(key_of[2], 3), 0, SLOTS - 1).astype(jnp.int32)
    lengths = draw_lengths(jax.random.fold_in(key_of[7], 71), 0)
    w_proj = normal_values(key_of[4], (D, 4 * HD), D ** -0.5, 0.375)
    w_out = normal_values(key_of[5], (HD, D), HD ** -0.5, 0.25)
    grad_out = normal_values(key_of[6], (BATCH, LEN, D), 1.0, 6.0, ((0, 64), (1, 2)))
    return {"item_table": item_table, "serve_rows": serve_rows, "token_slots": token_slots, "lengths": lengths, "w_proj": w_proj, "w_out": w_out, "grad_out": grad_out}


epsilon = 1e-05

def silu_slope(inputs):
    sigmoid_value = jax.nn.sigmoid(inputs)
    return sigmoid_value * (1.0 + inputs * (1.0 - sigmoid_value))

def normalize(inputs):
    centred = inputs - lax.optimization_barrier(jnp.mean(inputs, axis=-1, keepdims=True))
    inverse = lax.rsqrt(lax.optimization_barrier(jnp.mean(centred * centred, axis=-1, keepdims=True)) + epsilon)
    return (centred * inverse, inverse)

def normalize_wide(inputs):
    middle = lax.optimization_barrier(jnp.mean(inputs, axis=-1, keepdims=True))
    square_mean = lax.optimization_barrier(jnp.mean(inputs * inputs, axis=-1, keepdims=True))
    inverse = lax.rsqrt(square_mean - middle * middle + epsilon)
    return ((inputs - middle) * inverse, inverse)

def norm_back(gradients, normed, inverse):
    return (gradients - lax.optimization_barrier(jnp.mean(gradients, axis=-1, keepdims=True)) - normed * lax.optimization_barrier(jnp.mean(gradients * normed, axis=-1, keepdims=True))) * inverse

def rounded(inputs):
    return lax.optimization_barrier(inputs.astype(jnp.bfloat16)).astype(jnp.float32)

def per_history(embedded, cotangent, length, w_proj, w_out):
    positions = jnp.arange(LEN, dtype=jnp.int32)
    valid_rows = positions < length
    normal_x, input_inverse = normalize(embedded)
    normed_input = normal_x.astype(jnp.bfloat16)
    pre_act = jnp.dot(normed_input, w_proj, preferred_element_type=jnp.float32)
    activated = jax.nn.silu(pre_act).astype(jnp.bfloat16)
    gating, values, queries, keyrows = jnp.split(activated, 4, axis=1)
    score_scale = HEAD ** (-0.5)
    heads_q = queries.astype(jnp.float32).reshape(LEN, HEADS, HEAD)
    heads_k = keyrows.astype(jnp.float32).reshape(LEN, HEADS, HEAD)
    heads_v = values.astype(jnp.float32).reshape(LEN, HEADS, HEAD)
    allowed = ((positions[None, :] <= positions[:, None]) & (positions[None, :] < length)).astype(jnp.float32)
    scaled = jnp.einsum('ihd,jhd->hij', heads_q, heads_k) * score_scale
    weights = rounded(jax.nn.silu(scaled) * allowed)
    attended = jnp.einsum('hij,jhd->ihd', weights, heads_v).reshape(LEN, HD)
    normed_out, out_inverse = normalize_wide(attended)
    gated_rows = (normed_out * gating.astype(jnp.float32)).astype(jnp.bfloat16)
    mixed_rows = jnp.dot(gated_rows, w_out, preferred_element_type=jnp.float32)
    layer_out = jnp.where(valid_rows[:, None], embedded + mixed_rows, 0.0).astype(jnp.bfloat16)
    masked_g = jnp.where(valid_rows[:, None], cotangent, jnp.zeros_like(cotangent))
    grad_gated = jnp.dot(masked_g, w_out.T, preferred_element_type=jnp.float32)
    grad_gating = grad_gated * normed_out
    grad_attended = rounded(norm_back(grad_gated * gating.astype(jnp.float32), normed_out, out_inverse))
    heads_g = grad_attended.reshape(LEN, HEADS, HEAD)
    grad_weights = jnp.einsum('ihd,jhd->hij', heads_g, heads_v)
    grad_scores = rounded(grad_weights * silu_slope(scaled) * score_scale * allowed)
    grad_q = jnp.einsum('hij,jhd->ihd', grad_scores, heads_k).reshape(LEN, HD)
    grad_k = jnp.einsum('hij,ihd->jhd', grad_scores, heads_q).reshape(LEN, HD)
    grad_v = jnp.einsum('hij,ihd->jhd', weights, heads_g).reshape(LEN, HD)
    grad_act = jnp.concatenate([grad_gating, grad_v, grad_q, grad_k], axis=1)
    grad_pre = (grad_act * silu_slope(pre_act)).astype(jnp.bfloat16)
    grad_x = jnp.dot(grad_pre, w_proj.T, preferred_element_type=jnp.float32)
    grad_emb = masked_g.astype(jnp.float32) + norm_back(grad_x, normal_x, input_inverse)
    return (layer_out, grad_emb)

def reference(item_table, serve_rows, token_slots, lengths, w_proj, w_out, grad_out):
    served_rows = serve_rows.reshape(BATCH, BATCH, LEN // TOK_DEV, CAP)
    owner_index = token_slots // CAP
    within = token_slots % CAP
    shard_index = (jnp.arange(LEN, dtype=jnp.int32) // TOK_DEV)[None, :, None]
    batch_index = jnp.arange(BATCH, dtype=jnp.int32)[:, None, None]
    row_ids = (owner_index * ROWS_DEV + served_rows[owner_index, batch_index, shard_index, within]).astype(jnp.int32)
    embedded = item_table[row_ids[..., 0]]
    for feature in range(1, FEATS):
        embedded = embedded + item_table[row_ids[..., feature]]

    def one_history(items):
        return per_history(items[0], items[1], items[2], w_proj, w_out)
    layer_out, grad_emb = lax.map(one_history, (embedded, grad_out, lengths))
    flat_grads = grad_emb.reshape(-1, D)
    grad_table = jnp.zeros((TABLE_ROWS, D), jnp.float32)
    for feature in range(FEATS):
        grad_table = grad_table + jax.ops.segment_sum(flat_grads, row_ids[..., feature].reshape(-1), num_segments=TABLE_ROWS)
    return (layer_out, grad_table)
```

```python
import functools

import jax
import jax.numpy as jnp
from jax import lax
from jax.experimental import pallas as pl
from jax.experimental.pallas import tpu as pltpu
from jax.sharding import PartitionSpec as P

HEAD = 128
EPS = 1e-05
SCALE = HEAD**-0.5
MESH = pl.DeviceIdType.MESH
F32 = jnp.float32
BF16 = jnp.bfloat16
NN = (((1,), (0,)), ((), ()))
NT = (((1,), (1,)), ((), ()))
TN = (((0,), (0,)), ((), ()))


def dot(a, b, form=NN):
    return lax.dot_general(a, b, form, preferred_element_type=F32)


def iota(shape, dim):
    return lax.broadcasted_iota(jnp.int32, shape, dim)


def place(step, lane, side, sign):
    me = lax.axis_index("table")
    z, y, x = me // (side * side), (me // side) % side, me % side
    dz, dy, dx = lane, (step // side + lane) % side, (step + lane) % side
    if sign > 0:
        z, y, x = (z + dz) % side, (y + dy) % side, (x + dx) % side
    else:
        z, y, x = (z - dz + side) % side, (y - dy + side) % side, (x - dx + side) % side
    return (z * side + y) * side + x


def greet_all(side):
    barrier = pltpu.get_barrier_semaphore()
    core = lax.axis_index("ctx")

    def greet(step, lane):
        pl.semaphore_signal(
            barrier, inc=1, device_id=(place(step, lane, side, 1), core), device_id_type=MESH
        )

    for lane in range(1, side):
        greet(0, lane)

    @pl.loop(1, side * side)
    def _(step):
        for lane in range(side):
            greet(step, lane)


def exchange(send, recv, send_sem, recv_sem, step, lane, side, cap):
    row = pl.multiple_of((step * side + lane) * cap, cap)
    return pltpu.make_async_remote_copy(
        src_ref=send.at[pl.ds(row, cap)],
        dst_ref=recv.at[pl.ds(row, cap)],
        send_sem=send_sem.at[step * side + lane],
        recv_sem=recv_sem.at[step * side + lane],
        device_id=(place(step, lane, side, 1), lax.axis_index("ctx")),
        device_id_type=MESH,
    )


def for_steps(side, body):
    body(0, 1)

    @pl.loop(1, side * side)
    def _(step):
        body(step, 0)


def multi_hot(slots_ref, base, rows, columns):
    row = iota((rows, columns), 0) + base
    total = jnp.zeros((rows, columns), F32)
    for feature in range(slots_ref.shape[0]):
        total = total + jnp.where(slots_ref[pl.ds(feature, 1), :] == row, 1.0, 0.0)
    return total.astype(BF16)


def fetch_kernel(
    side, cap, table, serve, slots, out, rounded, picked, send, recv, hot, total, send_sem, recv_sem
):
    greet_all(side)
    lanes = side * cap
    table_rows = table.shape[0]
    rounded[...] = table[...].astype(BF16)
    square = iota((cap, cap), 0) == iota((cap, cap), 1)
    columns = iota((cap, table_rows), 1)

    def pick(step):
        for lane in range(side):
            ids = serve[pl.ds(place(step, lane, side, 1), 1), :]
            ids = jnp.sum(jnp.where(square, ids.astype(F32), 0.0), axis=1, keepdims=True)
            one_hot = jnp.where(ids.astype(jnp.int32) == columns, 1.0, 0.0)
            picked[lane * cap : (lane + 1) * cap, :] = one_hot.astype(BF16)
        row = pl.multiple_of(step * lanes, lanes)
        send[pl.ds(row, lanes), :] = dot(picked[...], rounded[...]).astype(BF16)

    pick(0)
    pl.semaphore_wait(pltpu.get_barrier_semaphore(), side**3 - 1)
    recv[0:cap, :] = send[0:cap, :]

    def start(step, first):
        for lane in range(first, side):
            exchange(send, recv, send_sem, recv_sem, step, lane, side, cap).start()

    start(0, 1)

    @pl.loop(1, side * side)
    def _(step):
        pick(step)
        start(step, 0)

    positions = slots.shape[1]

    @pl.loop(0, side * side)
    def _(step):
        for lane in range(side):
            base = place(step, lane, side, -1) * cap
            row = pl.multiple_of((step * side + lane) * cap, cap)
            hot[pl.ds(row, cap), :] = multi_hot(slots, base, cap, positions)

    total[...] = jnp.zeros_like(total)

    def take(step, first):
        for lane in range(first, side):
            exchange(send, recv, send_sem, recv_sem, step, lane, side, cap).wait_recv()
        row = pl.multiple_of(step * lanes, lanes)
        total[...] += dot(recv[pl.ds(row, lanes), :], hot[pl.ds(row, lanes), :], TN)

    for_steps(side, take)
    out[...] = total[...].T

    def sent(step, first):
        for lane in range(first, side):
            exchange(send, recv, send_sem, recv_sem, step, lane, side, cap).wait_send()

    for_steps(side, sent)


def fetch(side, item_table, serve_rows, slots):
    cap = serve_rows.shape[1]
    chips = side**3
    rows, width = item_table.shape
    positions = slots.shape[1]
    whole = pl.BlockSpec(memory_space=pltpu.VMEM)
    return pl.pallas_call(
        functools.partial(fetch_kernel, side, cap),
        out_shape=jax.ShapeDtypeStruct((positions, width), F32),
        in_specs=[whole] * 3,
        out_specs=whole,
        scratch_shapes=[
            pltpu.VMEM((rows, width), BF16),
            pltpu.VMEM((side * cap, rows), BF16),
            pltpu.VMEM((chips * cap, width), BF16),
            pltpu.VMEM((chips * cap, width), BF16),
            pltpu.VMEM((chips * cap, positions), BF16),
            pltpu.VMEM((width, positions), F32),
            pltpu.SemaphoreType.DMA((chips,)),
            pltpu.SemaphoreType.DMA((chips,)),
        ],
        compiler_params=pltpu.CompilerParams(
            collective_id=0, has_side_effects=True, vmem_limit_bytes=48 << 20
        ),
        name="fetch",
    )(item_table, serve_rows, slots)


def give_kernel(
    side, cap, grads, slots, serve, out,
    send, recv, total, half_send, half_recv, send_sem, recv_sem, half_sem,
):
    greet_all(side)
    table, core = lax.axis_index("table"), lax.axis_index("ctx")
    barrier = pltpu.get_barrier_semaphore()
    other = (table, 1 - core)
    pl.semaphore_signal(barrier, inc=1, device_id=other, device_id_type=MESH)
    lanes = side * cap
    positions = slots.shape[1]
    rows = total.shape[0]
    total[...] = jnp.zeros_like(total)

    def sums(step):
        for lane in range(side):
            base = place(step, lane, side, 1) * cap
            row = pl.multiple_of((step * side + lane) * cap, cap)
            send[pl.ds(row, cap), :] = dot(
                multi_hot(slots, base, cap, positions), grads[...]
            ).astype(BF16)

    sums(0)
    pl.semaphore_wait(barrier, side**3)
    recv[0:cap, :] = send[0:cap, :]

    def start(step, first):
        for lane in range(first, side):
            exchange(send, recv, send_sem, recv_sem, step, lane, side, cap).start()

    start(0, 1)

    @pl.loop(1, side * side)
    def _(step):
        sums(step)
        start(step, 0)

    def add(step, first):
        ids = [serve[pl.ds(place(step, lane, side, -1), 1), :] for lane in range(side)]
        one_hot = jnp.where(
            jnp.concatenate(ids, axis=1) == iota((rows, lanes), 0), 1.0, 0.0
        ).astype(BF16)
        for lane in range(first, side):
            exchange(send, recv, send_sem, recv_sem, step, lane, side, cap).wait_recv()
        row = pl.multiple_of(step * lanes, lanes)
        total[...] += dot(one_hot, recv[pl.ds(row, lanes), :])

    for_steps(side, add)
    half = rows // 2
    mine = pl.ds(pl.multiple_of(core * half, half), half)
    theirs = pl.ds(pl.multiple_of((1 - core) * half, half), half)
    half_send[...] = total[theirs, :].astype(BF16)
    swap = pltpu.make_async_remote_copy(
        src_ref=half_send,
        dst_ref=half_recv,
        send_sem=half_sem.at[0],
        recv_sem=half_sem.at[1],
        device_id=other,
        device_id_type=MESH,
    )
    swap.start()

    def sent(step, first):
        for lane in range(first, side):
            exchange(send, recv, send_sem, recv_sem, step, lane, side, cap).wait_send()

    for_steps(side, sent)
    swap.wait()
    out[...] = total[mine, :] + half_recv[...].astype(F32)


def give(side, grads, slots, serve_rows, rows):
    cap = serve_rows.shape[1]
    chips = side**3
    width = grads.shape[1]
    whole = pl.BlockSpec(memory_space=pltpu.VMEM)
    return pl.pallas_call(
        functools.partial(give_kernel, side, cap),
        out_shape=jax.ShapeDtypeStruct((rows // 2, width), F32),
        in_specs=[whole] * 3,
        out_specs=whole,
        scratch_shapes=[
            pltpu.VMEM((chips * cap, width), BF16),
            pltpu.VMEM((chips * cap, width), BF16),
            pltpu.VMEM((rows, width), F32),
            pltpu.VMEM((rows // 2, width), BF16),
            pltpu.VMEM((rows // 2, width), BF16),
            pltpu.SemaphoreType.DMA((chips,)),
            pltpu.SemaphoreType.DMA((chips,)),
            pltpu.SemaphoreType.DMA((2,)),
        ],
        compiler_params=pltpu.CompilerParams(
            collective_id=2, has_side_effects=True, vmem_limit_bytes=48 << 20
        ),
        name="give",
    )(grads, slots, serve_rows)


def layer_kernel(
    block, embedded, cotangent, lengths, w_proj, w_out, layer_out, grad_emb,
    x_all, g_all, weights_own, out_own, gate, value, query, keyrow, slope,
    grad_gated, attended, stat_send, stat_recv, soft, soft_slope, grad_att,
    grad_q, grad_k, grad_v, gated_own, gated_send, gated_recv, gx_own, gx_send, gx_recv,
    send_sem, recv_sem,
):
    table, core = lax.axis_index("table"), lax.axis_index("ctx")
    barrier = pltpu.get_barrier_semaphore()
    pl.semaphore_signal(barrier, inc=1, device_id=(table, 1 - core), device_id_type=MESH)
    rows, width = embedded.shape
    cols = value.shape[1]
    heads = cols // HEAD
    own_blocks = rows // block
    blocks = 2 * own_blocks
    length = lengths[0]

    def copy_over(src, dst, number):
        return pltpu.make_async_remote_copy(
            src_ref=src,
            dst_ref=dst,
            send_sem=send_sem.at[number],
            recv_sem=recv_sem.at[number],
            device_id=(table, 1 - core),
            device_id_type=MESH,
        )

    def rows_of(index):
        return pl.ds(pl.multiple_of(index * block, block), block)

    first = core * own_blocks
    start_cols = pl.multiple_of(core * cols, cols)

    def valid(index, height):
        return iota((height, 1), 0) + index * block < length

    def normalize(index):
        rows_x = embedded[rows_of(index), :]
        centred = rows_x - jnp.mean(rows_x, axis=-1, keepdims=True)
        inverse = lax.rsqrt(jnp.mean(centred * centred, axis=-1, keepdims=True) + EPS)
        return centred * inverse, inverse

    at_g, at_x = 0, own_blocks
    at_stat = 2 * own_blocks
    at_gated = at_stat + blocks
    at_gx = at_gated + own_blocks

    def send_x(index):
        here = rows_of(first + index)
        return copy_over(x_all.at[here], x_all.at[here], at_x + index)

    def send_g(index):
        here = rows_of(first + index)
        return copy_over(g_all.at[here], g_all.at[here], at_g + index)

    for index in range(own_blocks):
        x_all[rows_of(first + index), :] = normalize(index)[0].astype(BF16)
        if index == 0:
            pl.semaphore_wait(barrier, 1)
        send_x(index).start()
    for index in range(own_blocks):
        rows_g = cotangent[rows_of(index), :]
        g_all[rows_of(first + index), :] = jnp.where(
            valid(first + index, block), rows_g, jnp.zeros_like(rows_g)
        )
        send_g(index).start()
    for part in range(4):
        here = pl.multiple_of(part * 2 * cols + core * cols, cols)
        weights_own[part] = w_proj[:, pl.ds(here, cols)]
    out_own[...] = w_out[pl.ds(start_cols, cols), :]

    def project(index):
        here = rows_of(index)
        rows_x = x_all[here, :]
        for part, ref in enumerate((gate, value, query, keyrow)):
            h = dot(rows_x, weights_own[part]) * 0.5
            th = jnp.tanh(h)
            up = 1.0 + th
            act = h * up
            slope[here, part * cols : (part + 1) * cols] = 0.5 * (up + act * (1.0 - th))
            act = act.astype(BF16)
            if part == 1:
                act = jnp.where(valid(index, block), act, jnp.zeros_like(act))
            ref[here, :] = act

    def spread(index):
        here = rows_of(index)
        grad_gated[here, :] = dot(g_all[here, :], out_own[...], NT)

    @pl.loop(0, own_blocks)
    def _(index):
        project(first + index)
        spread(first + index)

    attended[...] = jnp.zeros_like(attended)
    grad_q[...] = jnp.zeros_like(grad_q)
    grad_k[...] = jnp.zeros_like(grad_k)
    grad_v[...] = jnp.zeros_like(grad_v)

    @pl.loop(0, own_blocks)
    def _(index):
        theirs = (1 - core) * own_blocks + index
        send_x(index).wait_recv()
        project(theirs)
        send_g(index).wait_recv()
        spread(theirs)

    def head(number):
        return slice(number * HEAD, (number + 1) * HEAD)

    def forward_pair(i, j, masked):
        slot = i % 2
        for number in range(heads):
            h = dot(query[rows_of(i), head(number)], keyrow[rows_of(j), head(number)], NT)
            h = h * (0.5 * SCALE)
            th = jnp.tanh(h)
            up = 1.0 + th
            act = h * up
            twice = up + act * (1.0 - th)
            if masked:
                allowed = iota((block, block), 1) <= iota((block, block), 0)
                act = jnp.where(allowed, act, 0.0)
                twice = jnp.where(allowed, twice, 0.0)
            act = act.astype(BF16)
            soft[slot, number, j] = act
            soft_slope[slot, number, j] = twice.astype(BF16)
            attended[rows_of(i), head(number)] += dot(act, value[rows_of(j), head(number)])

    def send_stat(i):
        return copy_over(stat_send.at[rows_of(i)], stat_recv.at[rows_of(i)], at_stat + i)

    def forward(i):
        @pl.loop(0, i)
        def _(j):
            forward_pair(i, j, False)

        forward_pair(i, i, True)
        here = rows_of(i)
        att = attended[here, :]
        t = grad_gated[here, :] * gate[here, :].astype(F32)
        lane = iota((block, 128), 1)
        sums = jnp.zeros((block, 128), F32)
        for number, term in enumerate((att, att * att, t, t * att)):
            sums = jnp.where(lane == number, jnp.sum(term, axis=1, keepdims=True), sums)
        stat_send[here, :] = sums
        send_stat(i).start()

    def is_own(i):
        return (i // own_blocks) == core

    def send_gated(index):
        here = rows_of(index)
        return copy_over(gated_send.at[here], gated_recv.at[here], at_gated + index)

    def send_gx(index):
        here = rows_of(index)
        return copy_over(gx_send.at[here], gx_recv.at[here], at_gx + index)

    def combine(i):
        here = rows_of(i)
        send_stat(i).wait_recv()
        mean = (stat_send[here, :] + stat_recv[here, :]) * (1.0 / (2 * cols))
        middle = mean[:, 0:1]
        inverse = lax.rsqrt(mean[:, 1:2] - middle * middle + EPS)
        mean_t = mean[:, 2:3]
        mean_tn = (mean[:, 3:4] - middle * mean_t) * inverse
        gates = gate[here, :].astype(F32)
        grads = grad_gated[here, :]
        normed = (attended[here, :] - middle) * inverse
        gated = (normed * gates).astype(BF16)
        grad_att[here, :] = ((grads * gates - mean_t - normed * mean_tn) * inverse).astype(BF16)
        grad_gated[here, :] = grads * normed
        local = rows_of(i % own_blocks)

        @pl.when(is_own(i))
        def _():
            gated_own[local, :] = gated

        @pl.when(jnp.logical_not(is_own(i)))
        def _():
            gated_send[local, :] = gated
            send_gated(i % own_blocks).start()

    def backward_pair(i, j):
        slot = i % 2
        for number in range(heads):
            at = head(number)
            grads = grad_att[rows_of(i), at]
            grad_p = dot(grads, value[rows_of(j), at], NT)
            grad_s = (grad_p * soft_slope[slot, number, j].astype(F32)).astype(BF16)
            grad_v[rows_of(j), at] += dot(soft[slot, number, j], grads, TN)
            grad_k[rows_of(j), at] += dot(grad_s, query[rows_of(i), at], TN)
            grad_q[rows_of(i), at] += dot(grad_s, keyrow[rows_of(j), at])

    def backward(i):
        combine(i)

        @pl.loop(0, i + 1)
        def _(j):
            backward_pair(i, j)

        here = rows_of(i)
        total = jnp.zeros((block, width), F32)
        for part in range(4):
            if part == 0:
                term = grad_gated[here, :]
            elif part == 1:
                term = jnp.where(valid(i, block), grad_v[here, :], 0.0)
            else:
                term = (grad_q, grad_k)[part - 2][here, :] * (0.5 * SCALE)
            term = (term * slope[here, part * cols : (part + 1) * cols]).astype(BF16)
            total = total + dot(term, weights_own[part], NT)
        local = rows_of(i % own_blocks)

        @pl.when(is_own(i))
        def _():
            gx_own[local, :] = total

        @pl.when(jnp.logical_not(is_own(i)))
        def _():
            gx_send[local, :] = total
            send_gx(i % own_blocks).start()

    forward(blocks - 1)

    @pl.loop(0, blocks - 1)
    def _(step):
        forward(blocks - 2 - step)
        backward(blocks - 1 - step)

    backward(0)

    for index in range(own_blocks):
        here = rows_of(index)
        send_gated(index).wait_recv()
        their_cols = pl.multiple_of((1 - core) * cols, cols)
        mixed = dot(gated_own[here, :], out_own[...]) + dot(
            gated_recv[here, :], w_out[pl.ds(their_cols, cols), :]
        )
        layer_out[here, :] = jnp.where(
            valid(first + index, block), embedded[here, :] + mixed, 0.0
        ).astype(BF16)
    for index in reversed(range(own_blocks)):
        here = rows_of(index)
        normal_x, inverse = normalize(index)
        send_gx(index).wait_recv()
        grad_x = gx_own[here, :] + gx_recv[here, :]
        middle = jnp.mean(grad_x, axis=-1, keepdims=True)
        along = jnp.mean(grad_x * normal_x, axis=-1, keepdims=True)
        masked = g_all[rows_of(first + index), :].astype(F32)
        grad_emb[here, :] = (masked + (grad_x - middle - normal_x * along) * inverse).astype(BF16)
    for index in range(own_blocks):
        send_x(index).wait_send()
        send_g(index).wait_send()
        send_gated(index).wait_send()
        send_gx(index).wait_send()

    @pl.loop(0, blocks)
    def _(i):
        send_stat(i).wait_send()


def layer(embedded, cotangent, lengths, w_proj, w_out, block):
    rows, width = embedded.shape
    total = 2 * rows
    cols = w_out.shape[0] // 2
    heads = cols // HEAD
    own_blocks = rows // block
    blocks = 2 * own_blocks
    copies = 4 * own_blocks + blocks
    whole = pl.BlockSpec(memory_space=pltpu.VMEM)
    wide_b, wide_f = pltpu.VMEM((total, cols), BF16), pltpu.VMEM((total, cols), F32)
    pairs = pltpu.VMEM((2, heads, blocks, block, block), BF16)
    return pl.pallas_call(
        functools.partial(layer_kernel, block),
        out_shape=(
            jax.ShapeDtypeStruct((rows, width), BF16),
            jax.ShapeDtypeStruct((rows, width), BF16),
        ),
        in_specs=[whole, whole, pl.BlockSpec(memory_space=pltpu.SMEM), whole, whole],
        out_specs=(whole, whole),
        scratch_shapes=[
            pltpu.VMEM((total, width), BF16),
            pltpu.VMEM((total, width), BF16),
            pltpu.VMEM((4, width, cols), BF16),
            pltpu.VMEM((cols, width), BF16),
            wide_b,
            wide_b,
            wide_b,
            wide_b,
            pltpu.VMEM((total, 4 * cols), F32),
            wide_f,
            wide_f,
            pltpu.VMEM((total, 128), F32),
            pltpu.VMEM((total, 128), F32),
            pairs,
            pairs,
            wide_b,
            wide_f,
            wide_f,
            wide_f,
            pltpu.VMEM((rows, cols), BF16),
            pltpu.VMEM((rows, cols), BF16),
            pltpu.VMEM((rows, cols), BF16),
            pltpu.VMEM((rows, width), F32),
            pltpu.VMEM((rows, width), F32),
            pltpu.VMEM((rows, width), F32),
            pltpu.SemaphoreType.DMA((copies,)),
            pltpu.SemaphoreType.DMA((copies,)),
        ],
        compiler_params=pltpu.CompilerParams(
            collective_id=1, has_side_effects=True, vmem_limit_bytes=62 << 20
        ),
        name="layer",
    )(embedded, cotangent, lengths, w_proj, w_out)


def on_device(side, item_table, serve_rows, token_slots, lengths, w_proj, w_out, grad_out):
    slots = token_slots[0].T
    embedded = fetch(side, item_table, serve_rows, slots)
    layer_out, grad_emb = layer(
        embedded, grad_out[0], lengths, w_proj, w_out, min(512, embedded.shape[0])
    )
    grad_table = give(side, grad_emb, slots, serve_rows, item_table.shape[0])
    return (layer_out[None], grad_table)


def solution(mesh):
    placed = (
        P("table", None),
        P("table", "ctx"),
        P("table", "ctx", None),
        P("table"),
        P(),
        P(),
        P("table", "ctx", None),
    )
    side = round(mesh.shape["table"] ** (1 / 3))
    return jax.shard_map(
        functools.partial(on_device, side),
        mesh=mesh,
        in_specs=placed,
        out_specs=(P("table", "ctx", None), P(("table", "ctx"), None)),
        check_vma=False,
    )
```

```python
import functools

import jax
import jax.numpy as jnp
from jax import lax
from jax.experimental import pallas as pl
from jax.experimental.pallas import tpu as pltpu
from jax.sharding import PartitionSpec as P

HEAD = 128
EPS = 1e-05
SCALE = HEAD**-0.5
MESH = pl.DeviceIdType.MESH
F32 = jnp.float32
BF16 = jnp.bfloat16
NN = (((1,), (0,)), ((), ()))
NT = (((1,), (1,)), ((), ()))
TN = (((0,), (0,)), ((), ()))


def dot(a, b, form=NN):
    return lax.dot_general(a, b, form, preferred_element_type=F32)


def iota(shape, dim):
    return lax.broadcasted_iota(jnp.int32, shape, dim)


def place(step, lane, side, sign):
    me = lax.axis_index("table")
    z, y, x = me // (side * side), (me // side) % side, me % side
    dz, dy, dx = lane, (step // side + lane) % side, (step + lane) % side
    if sign > 0:
        z, y, x = (z + dz) % side, (y + dy) % side, (x + dx) % side
    else:
        z, y, x = (z - dz + side) % side, (y - dy + side) % side, (x - dx + side) % side
    return (z * side + y) * side + x


def greet_all(side):
    barrier = pltpu.get_barrier_semaphore()
    core = lax.axis_index("ctx")

    def greet(step, lane):
        pl.semaphore_signal(
            barrier, inc=1, device_id=(place(step, lane, side, 1), core), device_id_type=MESH
        )

    for lane in range(1, side):
        greet(0, lane)

    @pl.loop(1, side * side)
    def _(step):
        for lane in range(side):
            greet(step, lane)


def exchange(side, cap, send, recv, send_sem, recv_sem, step, lane):
    row = pl.multiple_of((step * side + lane) * cap, cap)
    return pltpu.make_async_remote_copy(
        src_ref=send.at[pl.ds(row, cap)],
        dst_ref=recv.at[pl.ds(row, cap)],
        send_sem=send_sem.at[step * side + lane],
        recv_sem=recv_sem.at[step * side + lane],
        device_id=(place(step, lane, side, 1), lax.axis_index("ctx")),
        device_id_type=MESH,
    )


def for_steps(side, body):
    body(0, 1)

    @pl.loop(1, side * side)
    def _(step):
        body(step, 0)


def multi_hot(slots_ref, base, rows, start, columns):
    row = iota((rows, columns), 0) + base
    total = jnp.zeros((rows, columns), F32)
    for feature in range(slots_ref.shape[0]):
        total = total + jnp.where(slots_ref[feature : feature + 1, start : start + columns] == row, 1.0, 0.0)
    return total.astype(BF16)


def kernel(
    side, cap, block,
    table_in, serve_in, slots_in, lengths, w_proj_in, w_out_in, cotangent_in,
    layer_out, grad_table,
    serve, slots, weights_own, w_out, cotangent, picked, send, recv, back, turned, embedded,
    x_all, g_all, gate, value, query, keyrow, slope, grad_gated, attended, stat_send, stat_recv,
    soft, soft_slope, grad_att, grad_q, grad_k, grad_v, gated_own, gated_send, gated_recv,
    gx_own, gx_send, gx_recv, grads, half_send, half_recv, result,
    load_sem, store_sem, out_sem, in_sem, back_out_sem, back_in_sem, core_out_sem, core_in_sem,
):
    table, core = lax.axis_index("table"), lax.axis_index("ctx")
    other = (table, 1 - core)
    barrier = pltpu.get_barrier_semaphore()
    steps = side * side
    lanes = side * cap
    table_rows, width = grad_k.shape
    positions = slots.shape[1]
    cols = value.shape[1]
    heads = cols // HEAD
    own_blocks = positions // block
    blocks = 2 * own_blocks
    first = core * own_blocks
    length = lengths[0]
    own_cols = pl.multiple_of(core * cols, cols)
    their_cols = pl.multiple_of((1 - core) * cols, cols)

    loads = [(serve_in, serve), (table_in, grad_k), (slots_in, slots), (cotangent_in, cotangent)]
    for part in range(4):
        here = pl.multiple_of(part * 2 * cols + core * cols, cols)
        loads.append((w_proj_in.at[:, pl.ds(here, cols)], weights_own.at[part]))
    loads.append((w_out_in, w_out))
    loads = [
        pltpu.make_async_copy(src, dst, load_sem.at[number])
        for number, (src, dst) in enumerate(loads)
    ]
    for load in loads:
        load.start()
    greet_all(side)
    pl.semaphore_signal(barrier, inc=1, device_id=other, device_id_type=MESH)

    rounded = keyrow
    loads[0].wait()
    loads[1].wait()
    rounded[...] = grad_k[...].astype(BF16)
    square = iota((cap, cap), 0) == iota((cap, cap), 1)
    columns = iota((cap, table_rows), 1)

    def pick(step):
        for lane in range(side):
            ids = serve[pl.ds(place(step, lane, side, 1), 1), :]
            ids = jnp.sum(jnp.where(square, ids.astype(F32), 0.0), axis=1, keepdims=True)
            one_hot = jnp.where(ids.astype(jnp.int32) == columns, 1.0, 0.0)
            picked[lane * cap : (lane + 1) * cap, :] = one_hot.astype(BF16)
        row = pl.multiple_of(step * lanes, lanes)
        send[pl.ds(row, lanes), :] = dot(picked[...], rounded[...]).astype(BF16)

    ask = functools.partial(exchange, side, cap, send, recv, out_sem, in_sem)

    def start_ask(step, first_lane):
        for lane in range(first_lane, side):
            ask(step, lane).start()

    pick(0)
    pl.semaphore_wait(barrier, side**3)
    recv[0:cap, :] = send[0:cap, :]
    start_ask(0, 1)

    @pl.loop(1, steps)
    def _(step):
        pick(step)
        start_ask(step, 0)

    for load in loads[2:]:
        load.wait()

    def rows_of(index):
        return pl.ds(pl.multiple_of(index * block, block), block)

    def valid(index, height):
        return iota((height, 1), 0) + index * block < length

    def copy_over(src, dst, number):
        return pltpu.make_async_remote_copy(
            src_ref=src,
            dst_ref=dst,
            send_sem=core_out_sem.at[number],
            recv_sem=core_in_sem.at[number],
            device_id=other,
            device_id_type=MESH,
        )

    at_g, at_x = 0, own_blocks
    at_stat = 2 * own_blocks
    at_gated = at_stat + blocks
    at_gx = at_gated + own_blocks
    at_half = at_gx + own_blocks

    def send_x(index):
        here = rows_of(first + index)
        return copy_over(x_all.at[here], x_all.at[here], at_x + index)

    def send_g(index):
        here = rows_of(first + index)
        return copy_over(g_all.at[here], g_all.at[here], at_g + index)

    for index in range(own_blocks):
        rows_g = cotangent[rows_of(index), :]
        g_all[rows_of(first + index), :] = jnp.where(
            valid(first + index, block), rows_g, jnp.zeros_like(rows_g)
        )
        send_g(index).start()
    grad_k[...] = jnp.zeros_like(grad_k)
    grad_v[...] = jnp.zeros_like(grad_v)
    turned[...] = jnp.zeros_like(turned)

    def hot_rows(index, row, count):
        return pl.ds(pl.multiple_of(index * steps * lanes + row, cap), count)

    @pl.loop(0, steps)
    def _(step):
        for lane in range(side):
            base = place(step, lane, side, -1) * cap
            row = pl.multiple_of((step * side + lane) * cap, cap)
            for index in range(own_blocks):
                soft[hot_rows(index, row, cap), :] = multi_hot(slots, base, cap, index * block, block)

    for index in range(own_blocks):
        send_g(index).wait_recv()

    def take(step, first_lane):
        for lane in range(first_lane, side):
            ask(step, lane).wait_recv()
        row = pl.multiple_of(step * lanes, lanes)
        for index in range(own_blocks):
            turned[:, index * block : (index + 1) * block] += dot(
                recv[pl.ds(row, lanes), :], soft[hot_rows(index, row, lanes), :], TN
            )

    for_steps(side, take)
    embedded[...] = turned[...].T

    def normalize(index):
        rows_x = embedded[rows_of(index), :]
        centred = rows_x - jnp.mean(rows_x, axis=-1, keepdims=True)
        inverse = lax.rsqrt(jnp.mean(centred * centred, axis=-1, keepdims=True) + EPS)
        return centred * inverse, inverse

    for index in range(own_blocks):
        x_all[rows_of(first + index), :] = normalize(index)[0].astype(BF16)
        send_x(index).start()

    def project(index):
        here = rows_of(index)
        rows_x = x_all[here, :]
        for part, ref in enumerate((gate, value, query, keyrow)):
            h = dot(rows_x, weights_own[part]) * 0.5
            th = jnp.tanh(h)
            up = 1.0 + th
            act = h * up
            slope[here, part * cols : (part + 1) * cols] = (
                0.5 * (up + act * (1.0 - th))
            ).astype(BF16)
            act = act.astype(BF16)
            if part == 1:
                act = jnp.where(valid(index, block), act, jnp.zeros_like(act))
            ref[here, :] = act

    @pl.loop(0, own_blocks)
    def _(index):
        project(first + index)

    @pl.loop(0, own_blocks)
    def _(index):
        send_x(index).wait_recv()
        project((1 - core) * own_blocks + index)

    def head(number):
        return slice(number * HEAD, (number + 1) * HEAD)

    def pair_ref(ref, i, number, j):
        row = (((i % 2) * heads + number) * blocks + j) * block
        return ref.at[pl.ds(pl.multiple_of(row, block), block)]

    def forward_pair(i, j, masked):
        for number in range(heads):
            h = dot(query[rows_of(i), head(number)], keyrow[rows_of(j), head(number)], NT)
            h = h * (0.5 * SCALE)
            th = jnp.tanh(h)
            up = 1.0 + th
            act = h * up
            twice = up + act * (1.0 - th)
            if masked:
                allowed = iota((block, block), 1) <= iota((block, block), 0)
                act = jnp.where(allowed, act, 0.0)
                twice = jnp.where(allowed, twice, 0.0)
            act = act.astype(BF16)
            pair_ref(soft, i, number, j)[...] = act
            pair_ref(soft_slope, i, number, j)[...] = twice.astype(BF16)
            added = dot(act, value[rows_of(j), head(number)])
            if masked:
                attended[i % 2, :, head(number)] = added
            else:
                attended[i % 2, :, head(number)] += added

    def send_stat(i):
        return copy_over(stat_send.at[rows_of(i)], stat_recv.at[rows_of(i)], at_stat + i)

    def forward(i):
        forward_pair(i, i, True)
        here = rows_of(i)
        grad_gated[i % 2] = dot(g_all[here, :], w_out[pl.ds(own_cols, cols), :], NT)

        @pl.loop(0, i)
        def _(j):
            forward_pair(i, j, False)

        att = attended[i % 2]
        t = grad_gated[i % 2] * gate[here, :].astype(F32)
        lane = iota((block, 128), 1)
        sums = jnp.zeros((block, 128), F32)
        for number, term in enumerate((att, att * att, t, t * att)):
            sums = jnp.where(lane == number, jnp.sum(term, axis=1, keepdims=True), sums)
        stat_send[here, :] = sums
        send_stat(i).start()

    def is_own(i):
        return (i // own_blocks) == core

    def send_gated(index):
        here = rows_of(index)
        return copy_over(gated_send.at[here], gated_recv.at[here], at_gated + index)

    def send_gx(index):
        here = rows_of(index)
        return copy_over(gx_send.at[here], gx_recv.at[here], at_gx + index)

    def combine(i):
        here = rows_of(i)
        send_stat(i).wait_recv()
        mean = (stat_send[here, :] + stat_recv[here, :]) * (1.0 / (2 * cols))
        middle = mean[:, 0:1]
        inverse = lax.rsqrt(mean[:, 1:2] - middle * middle + EPS)
        mean_t = mean[:, 2:3]
        mean_tn = (mean[:, 3:4] - middle * mean_t) * inverse
        gates = gate[here, :].astype(F32)
        grad_rows = grad_gated[i % 2]
        normed = (attended[i % 2] - middle) * inverse
        gated = (normed * gates).astype(BF16)
        grad_att[...] = ((grad_rows * gates - mean_t - normed * mean_tn) * inverse).astype(BF16)
        grad_gated[i % 2] = grad_rows * normed
        local = rows_of(i % own_blocks)

        @pl.when(is_own(i))
        def _():
            gated_own[local, :] = gated

        @pl.when(jnp.logical_not(is_own(i)))
        def _():
            gated_send[local, :] = gated
            send_gated(i % own_blocks).start()

    def backward_pair(i, j):
        for number in range(heads):
            at = head(number)
            grad_rows = grad_att[:, at]
            grad_p = dot(grad_rows, value[rows_of(j), at], NT)
            twice = pair_ref(soft_slope, i, number, j)[...]
            grad_s = (grad_p * twice.astype(F32)).astype(BF16)
            grad_v[rows_of(j), at] += dot(pair_ref(soft, i, number, j)[...], grad_rows, TN)
            grad_k[rows_of(j), at] += dot(grad_s, query[rows_of(i), at], TN)
            grad_q[:, at] += dot(grad_s, keyrow[rows_of(j), at])

    def backward(i):
        combine(i)
        grad_q[...] = jnp.zeros_like(grad_q)

        @pl.loop(0, i + 1)
        def _(j):
            backward_pair(i, j)

        here = rows_of(i)
        total = jnp.zeros((block, width), F32)
        for part in range(4):
            if part == 0:
                term = grad_gated[i % 2]
            elif part == 1:
                term = jnp.where(valid(i, block), grad_v[here, :], 0.0)
            elif part == 2:
                term = grad_q[...] * (0.5 * SCALE)
            else:
                term = grad_k[here, :] * (0.5 * SCALE)
            slopes = slope[here, part * cols : (part + 1) * cols].astype(F32)
            total = total + dot((term * slopes).astype(BF16), weights_own[part], NT)
        local = rows_of(i % own_blocks)

        @pl.when(is_own(i))
        def _():
            gx_own[local, :] = total

        @pl.when(jnp.logical_not(is_own(i)))
        def _():
            gx_send[local, :] = total
            send_gx(i % own_blocks).start()

    forward(blocks - 1)

    @pl.loop(0, blocks - 1)
    def _(step):
        forward(blocks - 2 - step)
        backward(blocks - 1 - step)

    backward(0)

    def mix(index):
        here = rows_of(index)
        send_gated(index).wait_recv()
        mixed = dot(gated_own[here, :], w_out[pl.ds(own_cols, cols), :]) + dot(
            gated_recv[here, :], w_out[pl.ds(their_cols, cols), :]
        )
        cotangent[here, :] = jnp.where(
            valid(first + index, block), embedded[here, :] + mixed, 0.0
        ).astype(BF16)

    for index in reversed(range(own_blocks)):
        here = rows_of(index)
        normal_x, inverse = normalize(index)
        send_gx(index).wait_recv()
        grad_x = gx_own[here, :] + gx_recv[here, :]
        middle = jnp.mean(grad_x, axis=-1, keepdims=True)
        along = jnp.mean(grad_x * normal_x, axis=-1, keepdims=True)
        masked = g_all[rows_of(first + index), :].astype(F32)
        grads[here, :] = (masked + (grad_x - middle - normal_x * along) * inverse).astype(BF16)

    def sent(step, first_lane):
        for lane in range(first_lane, side):
            ask(step, lane).wait_send()

    for_steps(side, sent)
    give = functools.partial(exchange, side, cap, send, back, back_out_sem, back_in_sem)

    def sums_back(step):
        for lane in range(side):
            base = place(step, lane, side, 1) * cap
            row = pl.multiple_of((step * side + lane) * cap, cap)
            send[pl.ds(row, cap), :] = dot(
                multi_hot(slots, base, cap, 0, positions), grads[...]
            ).astype(BF16)

    def start_give(step, first_lane):
        for lane in range(first_lane, side):
            give(step, lane).start()

    sums_back(0)
    back[0:cap, :] = send[0:cap, :]
    start_give(0, 1)

    @pl.loop(1, steps)
    def _(step):
        sums_back(step)
        start_give(step, 0)

    for index in range(own_blocks):
        mix(index)
    store = pltpu.make_async_copy(cotangent, layer_out, store_sem.at[0])
    store.start()
    total = grad_k
    total[...] = jnp.zeros_like(total)

    def add(step, first_lane):
        ids = [serve[pl.ds(place(step, lane, side, -1), 1), :] for lane in range(side)]
        one_hot = jnp.where(
            jnp.concatenate(ids, axis=1) == iota((table_rows, lanes), 0), 1.0, 0.0
        ).astype(BF16)
        for lane in range(first_lane, side):
            give(step, lane).wait_recv()
        row = pl.multiple_of(step * lanes, lanes)
        total[...] += dot(one_hot, back[pl.ds(row, lanes), :])

    for_steps(side, add)
    half = table_rows // 2
    mine = pl.ds(pl.multiple_of(core * half, half), half)
    theirs = pl.ds(pl.multiple_of((1 - core) * half, half), half)
    half_send[...] = total[theirs, :].astype(BF16)
    swap = copy_over(half_send, half_recv, at_half)
    swap.start()

    def given(step, first_lane):
        for lane in range(first_lane, side):
            give(step, lane).wait_send()

    for_steps(side, given)
    for index in range(own_blocks):
        send_x(index).wait_send()
        send_g(index).wait_send()
        send_gated(index).wait_send()
        send_gx(index).wait_send()

    @pl.loop(0, blocks)
    def _(i):
        send_stat(i).wait_send()

    swap.wait()
    result[...] = total[mine, :] + half_recv[...].astype(F32)
    last = pltpu.make_async_copy(result, grad_table, store_sem.at[1])
    last.start()
    store.wait()
    last.wait()


def on_device(side, item_table, serve_rows, token_slots, lengths, w_proj, w_out, grad_out):
    slots = token_slots[0].T
    cap = serve_rows.shape[1]
    chips = side**3
    table_rows, width = item_table.shape
    positions = slots.shape[1]
    block = min(512, positions)
    total = 2 * positions
    cols = w_out.shape[0] // 2
    heads = cols // HEAD
    own_blocks = positions // block
    blocks = 2 * own_blocks
    copies = 4 * own_blocks + blocks + 1
    anywhere = pl.BlockSpec(memory_space=pl.ANY)
    sems = pltpu.SemaphoreType.DMA

    def rows_b(rows, columns):
        return pltpu.VMEM((rows, columns), BF16)

    def rows_f(rows, columns):
        return pltpu.VMEM((rows, columns), F32)

    pairs = rows_b(2 * heads * blocks * block, block)
    scratch = {
        "serve": pltpu.VMEM(serve_rows.shape, jnp.int32),
        "slots": pltpu.VMEM(slots.shape, jnp.int32),
        "weights_own": pltpu.VMEM((4, width, cols), BF16),
        "w_out": pltpu.VMEM(w_out.shape, BF16),
        "cotangent": rows_b(positions, width),
        "picked": rows_b(side * cap, table_rows),
        "send": rows_b(chips * cap, width),
        "recv": rows_b(chips * cap, width),
        "back": rows_b(chips * cap, width),
        "turned": rows_f(width, positions),
        "embedded": rows_f(positions, width),
        "x_all": rows_b(total, width),
        "g_all": rows_b(total, width),
        "gate": rows_b(total, cols),
        "value": rows_b(total, cols),
        "query": rows_b(total, cols),
        "keyrow": rows_b(total, cols),
        "slope": rows_b(total, 4 * cols),
        "grad_gated": pltpu.VMEM((2, block, cols), F32),
        "attended": pltpu.VMEM((2, block, cols), F32),
        "stat_send": rows_f(total, 128),
        "stat_recv": rows_f(total, 128),
        "soft": pairs,
        "soft_slope": pairs,
        "grad_att": rows_b(block, cols),
        "grad_q": rows_f(block, cols),
        "grad_k": rows_f(total, cols),
        "grad_v": rows_f(total, cols),
        "gated_own": rows_b(positions, cols),
        "gated_send": rows_b(positions, cols),
        "gated_recv": rows_b(positions, cols),
        "gx_own": rows_f(positions, width),
        "gx_send": rows_f(positions, width),
        "gx_recv": rows_f(positions, width),
        "grads": rows_b(positions, width),
        "half_send": rows_b(table_rows // 2, width),
        "half_recv": rows_b(table_rows // 2, width),
        "result": rows_f(table_rows // 2, width),
        "load_sem": sems((9,)),
        "store_sem": sems((2,)),
        "out_sem": sems((chips,)),
        "in_sem": sems((chips,)),
        "back_out_sem": sems((chips,)),
        "back_in_sem": sems((chips,)),
        "core_out_sem": sems((copies,)),
        "core_in_sem": sems((copies,)),
    }
    layer_out, grad_table = pl.pallas_call(
        functools.partial(kernel, side, cap, block),
        out_shape=(
            jax.ShapeDtypeStruct((positions, width), BF16),
            jax.ShapeDtypeStruct((table_rows // 2, width), F32),
        ),
        in_specs=[anywhere] * 3 + [pl.BlockSpec(memory_space=pltpu.SMEM)] + [anywhere] * 3,
        out_specs=(anywhere, anywhere),
        scratch_shapes=list(scratch.values()),
        compiler_params=pltpu.CompilerParams(
            collective_id=0, has_side_effects=True, vmem_limit_bytes=63 << 20
        ),
        name="hstu",
    )(item_table, serve_rows, slots, lengths, w_proj, w_out, grad_out[0])
    return (layer_out[None], grad_table)


def solution(mesh):
    placed = (
        P("table", None),
        P("table", "ctx"),
        P("table", "ctx", None),
        P("table"),
        P(),
        P(),
        P("table", "ctx", None),
    )
    side = round(mesh.shape["table"] ** (1 / 3))
    return jax.shard_map(
        functools.partial(on_device, side),
        mesh=mesh,
        in_specs=placed,
        out_specs=(P("table", "ctx", None), P(("table", "ctx"), None)),
        check_vma=False,
    )
```

```python
import functools

import jax
import jax.numpy as jnp
from jax import lax
from jax.experimental import pallas as pl
from jax.experimental.pallas import tpu as pltpu
from jax.sharding import PartitionSpec as P

HEAD = 128
EPS = 1e-05
SCALE = HEAD**-0.5
MESH = pl.DeviceIdType.MESH
F32 = jnp.float32
BF16 = jnp.bfloat16
NN = (((1,), (0,)), ((), ()))
NT = (((1,), (1,)), ((), ()))
TN = (((0,), (0,)), ((), ()))


def dot(a, b, form=NN):
    return lax.dot_general(a, b, form, preferred_element_type=F32)


def iota(shape, dim):
    return lax.broadcasted_iota(jnp.int32, shape, dim)


def place(step, lane, side, sign):
    me = lax.axis_index("table")
    z, y, x = lax.div(me, side * side), lax.rem(lax.div(me, side), side), lax.rem(me, side)
    far = lax.div(step, side) if isinstance(step, jax.Array) else step // side
    if sign > 0:
        z, y, x = z + lane, y + far + step, x + step
    else:
        z, y, x = z - lane + side, y - far - step + side * (side + 1), x - step + side * side
    return (lax.rem(z, side) * side + lax.rem(y, side)) * side + lax.rem(x, side)


def greet_all(side):
    barrier = pltpu.get_barrier_semaphore()
    table, core = lax.axis_index("table"), lax.axis_index("ctx")

    def greet(chip, at):
        pl.semaphore_signal(barrier, inc=1, device_id=(chip, at), device_id_type=MESH)

    greet(table, 1 - core)
    for lane in range(1, side):
        greet(place(0, lane, side, 1), core)

    @pl.loop(1, side * side)
    def _(step):
        greet(place(step, 0, side, 1), core)


def hop_z(side, cap, send, relay, sems, step, lane):
    row = pl.multiple_of((step * side + lane) * cap, cap)
    return pltpu.make_async_remote_copy(
        src_ref=send.at[pl.ds(row, cap)],
        dst_ref=relay.at[pl.ds(row, cap)],
        send_sem=sems[0].at[step * side + lane],
        recv_sem=sems[1].at[step * side + lane],
        device_id=(place(0, lane, side, 1), lax.axis_index("ctx")),
        device_id_type=MESH,
    )


def hop_plane(side, cap, relay, recv, sems, step):
    row = pl.multiple_of(step * side * cap, side * cap)
    return pltpu.make_async_remote_copy(
        src_ref=relay.at[pl.ds(row, side * cap)],
        dst_ref=recv.at[pl.ds(row, side * cap)],
        send_sem=sems[2].at[step],
        recv_sem=sems[3].at[step],
        device_id=(place(step, 0, side, 1), lax.axis_index("ctx")),
        device_id_type=MESH,
    )


class Route:
    def __init__(self, side, cap, send, relay, recv, sems):
        self.side, self.cap, self.send, self.relay, self.recv = side, cap, send, relay, recv
        self.z = functools.partial(hop_z, side, cap, send, relay, sems)
        self.plane = functools.partial(hop_plane, side, cap, relay, recv, sems)

    def put(self, step, blocks):
        row = pl.multiple_of(step * self.side * self.cap, self.side * self.cap)
        self.relay[pl.ds(row, self.cap), :] = blocks[: self.cap]
        rest = pl.multiple_of(row + self.cap, self.cap)
        self.send[pl.ds(rest, (self.side - 1) * self.cap), :] = blocks[self.cap :]

    def start(self, step):
        for lane in range(1, self.side):
            self.z(step, lane).start()

    def arrive(self, step):
        for lane in range(1, self.side):
            self.z(step, lane).wait_recv()

    def pass_on(self, step):
        self.arrive(step)
        self.plane(step).start()

    def get(self, step):
        row = pl.multiple_of(step * self.side * self.cap, self.side * self.cap)
        return self.recv[pl.ds(row, self.side * self.cap), :]

    def finish(self):
        for lane in range(1, self.side):
            self.z(0, lane).wait_send()

        @pl.loop(1, self.side * self.side)
        def _(step):
            for lane in range(1, self.side):
                self.z(step, lane).wait_send()
            self.plane(step).wait_send()


def multi_hot(slots_ref, base, rows, start, columns):
    row = iota((rows, columns), 0) + base
    total = jnp.zeros((rows, columns), F32)
    for feature in range(slots_ref.shape[0]):
        total = total + jnp.where(slots_ref[feature : feature + 1, start : start + columns] == row, 1.0, 0.0)
    return total.astype(BF16)


def kernel(
    side, cap, block,
    table_in, serve_in, slots_in, lengths, w_proj_in, w_out_in, cotangent_in,
    layer_out, own_half, their_half,
    serve, slots, weights_own, w_out, cotangent, picked, send, relay, recv, back_relay, back,
    turned, embedded,
    x_all, g_all, gate, value, query, keyrow, slope, grad_gated, attended, stat_send, stat_recv,
    soft, soft_slope, grad_att, grad_q, grad_k, grad_v, gated_own, gated_send, gated_recv,
    gx_own, gx_send, gx_recv, grads, half_send,
    load_sem, store_sem, core_out_sem, core_in_sem, *route_sems,
):
    table, core = lax.axis_index("table"), lax.axis_index("ctx")
    other = (table, 1 - core)
    barrier = pltpu.get_barrier_semaphore()
    steps = side * side
    lanes = side * cap
    table_rows, width = grad_k.shape
    positions = slots.shape[1]
    cols = value.shape[1]
    heads = cols // HEAD
    own_blocks = positions // block
    blocks = 2 * own_blocks
    first = core * own_blocks
    length = lengths[0]
    own_cols = pl.multiple_of(core * cols, cols)
    their_cols = pl.multiple_of((1 - core) * cols, cols)

    loads = [(serve_in, serve), (table_in, grad_k), (slots_in, slots), (cotangent_in, cotangent)]
    for part in range(4):
        here = pl.multiple_of(part * 2 * cols + core * cols, cols)
        loads.append((w_proj_in.at[:, pl.ds(here, cols)], weights_own.at[part]))
    loads.append((w_out_in, w_out))
    loads = [
        pltpu.make_async_copy(src, dst, load_sem.at[number])
        for number, (src, dst) in enumerate(loads)
    ]
    for load in loads[:2]:
        load.start()
    greet_all(side)
    for load in loads[2:]:
        load.start()

    rounded = keyrow
    loads[0].wait()
    loads[1].wait()
    rounded[...] = grad_k[...].astype(BF16)
    square = iota((cap, cap), 0) == iota((cap, cap), 1)
    columns = iota((cap, table_rows), 1)

    def pick(step):
        for lane in range(side):
            ids = serve[pl.ds(place(step, lane, side, 1), 1), :]
            ids = jnp.sum(jnp.where(square, ids.astype(F32), 0.0), axis=1, keepdims=True)
            one_hot = jnp.where(ids.astype(jnp.int32) == columns, 1.0, 0.0)
            picked[lane * cap : (lane + 1) * cap, :] = one_hot.astype(BF16)
        ask.put(step, dot(picked[...], rounded[...]).astype(BF16))

    ask = Route(side, cap, send, relay, recv, route_sems[:4])
    early = 2
    for step in range(1, 1 + early):
        pick(step)
    pl.semaphore_wait(barrier, 1 + (side - 1) + (steps - 1))
    for step in range(1, 1 + early):
        ask.start(step)
    for load in loads[2:]:
        load.wait()

    def rows_of(index):
        if isinstance(index, int):
            return pl.ds(index * block, block)
        return pl.ds(pl.multiple_of(index * block, block), block)

    def valid(index, height):
        return iota((height, 1), 0) + index * block < length

    def copy_over(src, dst, number):
        return pltpu.make_async_remote_copy(
            src_ref=src,
            dst_ref=dst,
            send_sem=core_out_sem.at[number],
            recv_sem=core_in_sem.at[number],
            device_id=other,
            device_id_type=MESH,
        )

    at_g, at_x = 0, own_blocks
    at_stat = 2 * own_blocks
    at_gated = at_stat + blocks
    at_gx = at_gated + own_blocks
    at_half = at_gx + own_blocks

    def send_x(index):
        here = rows_of(first + index)
        return copy_over(x_all.at[here], x_all.at[here], at_x + index)

    def send_g(index):
        here = rows_of(first + index)
        return copy_over(g_all.at[here], g_all.at[here], at_g + index)

    for index in range(own_blocks):
        rows_g = cotangent[rows_of(index), :]
        g_all[rows_of(first + index), :] = jnp.where(
            valid(first + index, block), rows_g, jnp.zeros_like(rows_g)
        )
        send_g(index).start()
    grad_k[...] = jnp.zeros_like(grad_k)
    grad_v[...] = jnp.zeros_like(grad_v)
    turned[...] = jnp.zeros_like(turned)

    def hot_rows(index, row, count):
        return pl.ds(pl.multiple_of(index * steps * lanes + row, cap), count)

    def heat(step):
        for lane in range(side):
            base = place(step, lane, side, -1) * cap
            row = pl.multiple_of((step * side + lane) * cap, cap)
            for index in range(own_blocks):
                soft[hot_rows(index, row, cap), :] = multi_hot(slots, base, cap, index * block, block)

    def take(step, fetched):
        row = pl.multiple_of(step * lanes, lanes)
        for index in range(own_blocks):
            turned[:, index * block : (index + 1) * block] += dot(
                fetched, soft[hot_rows(index, row, lanes), :], TN
            )

    def take_far(step):
        ask.plane(step).wait_recv()
        take(step, ask.get(step))

    behind = 6

    @pl.loop(1 + early, steps)
    def _(step):
        pick(step)
        ask.start(step)
        heat(step - early)
        ask.pass_on(step - early)

        @pl.when(step > behind)
        def _():
            take_far(step - behind)

    pick(0)
    ask.start(0)
    for step in range(steps - early, steps):
        heat(step)
        ask.pass_on(step)
    heat(0)
    for index in range(own_blocks):
        send_g(index).wait_recv()

    @pl.loop(max(1, steps - behind), steps)
    def _(step):
        take_far(step)

    ask.arrive(0)
    take(0, relay[0:lanes, :])
    embedded[...] = turned[...].T

    def normalize(index):
        rows_x = embedded[rows_of(index), :]
        centred = rows_x - jnp.mean(rows_x, axis=-1, keepdims=True)
        inverse = lax.rsqrt(jnp.mean(centred * centred, axis=-1, keepdims=True) + EPS)
        return centred * inverse, inverse

    for index in range(own_blocks):
        x_all[rows_of(first + index), :] = normalize(index)[0].astype(BF16)
        send_x(index).start()

    def project(index):
        here = rows_of(index)
        rows_x = x_all[here, :]
        for part, ref in enumerate((gate, value, query, keyrow)):
            h = dot(rows_x, weights_own[part]) * 0.5
            th = jnp.tanh(h)
            up = 1.0 + th
            act = h * up
            slope[here, part * cols : (part + 1) * cols] = (
                0.5 * (up + act * (1.0 - th))
            ).astype(BF16)
            act = act.astype(BF16)
            if part == 1:
                act = jnp.where(valid(index, block), act, jnp.zeros_like(act))
            ref[here, :] = act

    @pl.loop(0, own_blocks)
    def _(index):
        project(first + index)

    @pl.loop(0, own_blocks)
    def _(index):
        send_x(index).wait_recv()
        project((1 - core) * own_blocks + index)

    def head(number):
        return slice(number * HEAD, (number + 1) * HEAD)

    def pair_ref(ref, i, number, j):
        row = (((i % 2) * heads + number) * blocks + j) * block
        return ref.at[pl.ds(row, block)]

    def forward_pair(i, j, masked):
        for number in range(heads):
            h = dot(query[rows_of(i), head(number)], keyrow[rows_of(j), head(number)], NT)
            h = h * (0.5 * SCALE)
            th = jnp.tanh(h)
            up = 1.0 + th
            act = h * up
            twice = up + act * (1.0 - th)
            if masked:
                allowed = iota((block, block), 1) <= iota((block, block), 0)
                act = jnp.where(allowed, act, 0.0)
                twice = jnp.where(allowed, twice, 0.0)
            act = act.astype(BF16)
            pair_ref(soft, i, number, j)[...] = act
            pair_ref(soft_slope, i, number, j)[...] = twice.astype(BF16)
            added = dot(act, value[rows_of(j), head(number)])
            if masked:
                attended[i % 2, :, head(number)] = added
            else:
                attended[i % 2, :, head(number)] += added

    def send_stat(i):
        return copy_over(stat_send.at[rows_of(i)], stat_recv.at[rows_of(i)], at_stat + i)

    def forward(i):
        forward_pair(i, i, True)
        here = rows_of(i)
        grad_gated[i % 2] = dot(g_all[here, :], w_out[pl.ds(own_cols, cols), :], NT)

        for j in range(i):
            forward_pair(i, j, False)

        att = attended[i % 2]
        t = grad_gated[i % 2] * gate[here, :].astype(F32)
        lane = iota((block, 128), 1)
        sums = jnp.zeros((block, 128), F32)
        for number, term in enumerate((att, att * att, t, t * att)):
            sums = jnp.where(lane == number, jnp.sum(term, axis=1, keepdims=True), sums)
        stat_send[here, :] = sums
        send_stat(i).start()

    def is_own(i):
        return (i // own_blocks) == core

    def send_gated(index):
        here = rows_of(index)
        return copy_over(gated_send.at[here], gated_recv.at[here], at_gated + index)

    def send_gx(index):
        here = rows_of(index)
        return copy_over(gx_send.at[here], gx_recv.at[here], at_gx + index)

    def combine(i):
        here = rows_of(i)
        send_stat(i).wait_recv()
        mean = (stat_send[here, :] + stat_recv[here, :]) * (1.0 / (2 * cols))
        middle = mean[:, 0:1]
        inverse = lax.rsqrt(mean[:, 1:2] - middle * middle + EPS)
        mean_t = mean[:, 2:3]
        mean_tn = (mean[:, 3:4] - middle * mean_t) * inverse
        gates = gate[here, :].astype(F32)
        grad_rows = grad_gated[i % 2]
        normed = (attended[i % 2] - middle) * inverse
        gated = (normed * gates).astype(BF16)
        grad_att[...] = ((grad_rows * gates - mean_t - normed * mean_tn) * inverse).astype(BF16)
        grad_gated[i % 2] = grad_rows * normed
        local = rows_of(i % own_blocks)

        @pl.when(is_own(i))
        def _():
            gated_own[local, :] = gated

        @pl.when(jnp.logical_not(is_own(i)))
        def _():
            gated_send[local, :] = gated
            send_gated(i % own_blocks).start()

    def backward_pair(i, j):
        for number in range(heads):
            at = head(number)
            grad_rows = grad_att[:, at]
            grad_p = dot(grad_rows, value[rows_of(j), at], NT)
            twice = pair_ref(soft_slope, i, number, j)[...]
            grad_s = (grad_p * twice.astype(F32)).astype(BF16)
            grad_v[rows_of(j), at] += dot(pair_ref(soft, i, number, j)[...], grad_rows, TN)
            grad_k[rows_of(j), at] += dot(grad_s, query[rows_of(i), at], TN)
            grad_q[:, at] += dot(grad_s, keyrow[rows_of(j), at])

    def backward(i):
        combine(i)
        grad_q[...] = jnp.zeros_like(grad_q)

        for j in range(i + 1):
            backward_pair(i, j)

        here = rows_of(i)
        total = jnp.zeros((block, width), F32)
        for part in range(4):
            if part == 0:
                term = grad_gated[i % 2]
            elif part == 1:
                term = jnp.where(valid(i, block), grad_v[here, :], 0.0)
            elif part == 2:
                term = grad_q[...] * (0.5 * SCALE)
            else:
                term = grad_k[here, :] * (0.5 * SCALE)
            slopes = slope[here, part * cols : (part + 1) * cols].astype(F32)
            total = total + dot((term * slopes).astype(BF16), weights_own[part], NT)
        local = rows_of(i % own_blocks)

        @pl.when(is_own(i))
        def _():
            gx_own[local, :] = total

        @pl.when(jnp.logical_not(is_own(i)))
        def _():
            gx_send[local, :] = total
            send_gx(i % own_blocks).start()

    forward(blocks - 1)

    for step in range(blocks - 1):
        forward(blocks - 2 - step)
        backward(blocks - 1 - step)

    backward(0)

    def mix(index):
        here = rows_of(index)
        send_gated(index).wait_recv()
        mixed = dot(gated_own[here, :], w_out[pl.ds(own_cols, cols), :]) + dot(
            gated_recv[here, :], w_out[pl.ds(their_cols, cols), :]
        )
        cotangent[here, :] = jnp.where(
            valid(first + index, block), embedded[here, :] + mixed, 0.0
        ).astype(BF16)

    for index in reversed(range(own_blocks)):
        here = rows_of(index)
        normal_x, inverse = normalize(index)
        send_gx(index).wait_recv()
        grad_x = gx_own[here, :] + gx_recv[here, :]
        middle = jnp.mean(grad_x, axis=-1, keepdims=True)
        along = jnp.mean(grad_x * normal_x, axis=-1, keepdims=True)
        masked = g_all[rows_of(first + index), :].astype(F32)
        grads[here, :] = (masked + (grad_x - middle - normal_x * along) * inverse).astype(BF16)

    ask.finish()
    give = Route(side, cap, send, back_relay, back, route_sems[4:])

    def sums_back(step):
        for lane in range(side):
            base = place(step, lane, side, 1) * cap
            picked[lane * cap : (lane + 1) * cap, 0:positions] = multi_hot(
                slots, base, cap, 0, positions
            )
        give.put(step, dot(picked[:, 0:positions], grads[...]).astype(BF16))
        give.start(step)

    total = grad_k

    def add(step, returned):
        ids = [serve[pl.ds(place(step, lane, side, -1), 1), :] for lane in range(side)]
        one_hot = jnp.where(
            jnp.concatenate(ids, axis=1) == iota((table_rows, lanes), 0), 1.0, 0.0
        ).astype(BF16)
        total[...] += dot(one_hot, returned)

    def add_far(step):
        give.plane(step).wait_recv()
        add(step, give.get(step))

    for step in range(1, 1 + early):
        sums_back(step)
    total[...] = jnp.zeros_like(total)

    @pl.loop(1 + early, steps)
    def _(step):
        sums_back(step)
        give.pass_on(step - early)

        @pl.when(step > behind)
        def _():
            add_far(step - behind)

    sums_back(0)
    for step in range(steps - early, steps):
        give.pass_on(step)
    for index in range(own_blocks):
        mix(index)
    store = pltpu.make_async_copy(cotangent, layer_out, store_sem.at[0])
    store.start()

    @pl.loop(max(1, steps - behind), steps)
    def _(step):
        add_far(step)

    give.arrive(0)
    add(0, back_relay[0:lanes, :])
    half = table_rows // 2
    mine = pl.ds(pl.multiple_of(core * half, half), half)
    theirs = pl.ds(pl.multiple_of((1 - core) * half, half), half)
    half_send[...] = total[theirs, :].astype(BF16)
    swap = copy_over(half_send, their_half, at_half)
    swap.start()
    last = pltpu.make_async_copy(total.at[mine], own_half, store_sem.at[1])
    last.start()

    give.finish()
    for index in range(own_blocks):
        send_x(index).wait_send()
        send_g(index).wait_send()
        send_gated(index).wait_send()
        send_gx(index).wait_send()

    @pl.loop(0, blocks)
    def _(i):
        send_stat(i).wait_send()

    store.wait()
    last.wait()
    swap.wait()


def finish_kernel(rows, own, their, rows_out, total_out, held, mine, theirs, load_sem, store_sem):
    half = own.shape[0] // 2
    loads = []
    for part in range(2):
        here = slice(part * half, (part + 1) * half)
        for number, (src, dst) in enumerate(((own, mine), (their, theirs))):
            loads.append(
                pltpu.make_async_copy(src.at[here], dst.at[here], load_sem.at[2 * part + number])
            )
    loads.append(pltpu.make_async_copy(rows, held, load_sem.at[4]))
    for load in loads:
        load.start()
    stores = []
    for part in range(2):
        here = slice(part * half, (part + 1) * half)
        loads[2 * part].wait()
        loads[2 * part + 1].wait()
        mine[here, :] = mine[here, :] + theirs[here, :].astype(F32)
        stores.append(pltpu.make_async_copy(mine.at[here], total_out.at[here], store_sem.at[part]))
        stores[-1].start()
    loads[4].wait()
    stores.append(pltpu.make_async_copy(held, rows_out, store_sem.at[2]))
    stores[-1].start()
    for store in stores:
        store.wait()


def finish(rows, own, their):
    anywhere = pl.BlockSpec(memory_space=pl.ANY)
    return pl.pallas_call(
        finish_kernel,
        out_shape=(
            jax.ShapeDtypeStruct(rows.shape, rows.dtype),
            jax.ShapeDtypeStruct(own.shape, own.dtype),
        ),
        in_specs=[anywhere] * 3,
        out_specs=(anywhere, anywhere),
        scratch_shapes=[
            pltpu.VMEM(rows.shape, rows.dtype),
            pltpu.VMEM(own.shape, own.dtype),
            pltpu.VMEM(their.shape, their.dtype),
            pltpu.SemaphoreType.DMA((5,)),
            pltpu.SemaphoreType.DMA((3,)),
        ],
        compiler_params=pltpu.CompilerParams(vmem_limit_bytes=63 << 20),
        name="finish",
    )(rows, own, their)


def on_device(side, item_table, serve_rows, token_slots, lengths, w_proj, w_out, grad_out):
    slots = token_slots[0].T
    cap = serve_rows.shape[1]
    chips = side**3
    table_rows, width = item_table.shape
    positions = slots.shape[1]
    block = min(512, positions)
    total = 2 * positions
    cols = w_out.shape[0] // 2
    heads = cols // HEAD
    own_blocks = positions // block
    blocks = 2 * own_blocks
    copies = 4 * own_blocks + blocks + 1
    anywhere = pl.BlockSpec(memory_space=pl.ANY)
    sems = pltpu.SemaphoreType.DMA

    def rows_b(rows, columns):
        return pltpu.VMEM((rows, columns), BF16)

    def rows_f(rows, columns):
        return pltpu.VMEM((rows, columns), F32)

    pairs = rows_b(2 * heads * blocks * block, block)
    scratch = {
        "serve": pltpu.VMEM(serve_rows.shape, jnp.int32),
        "slots": pltpu.VMEM(slots.shape, jnp.int32),
        "weights_own": pltpu.VMEM((4, width, cols), BF16),
        "w_out": pltpu.VMEM(w_out.shape, BF16),
        "cotangent": rows_b(positions, width),
        "picked": rows_b(side * cap, table_rows),
        "send": rows_b(chips * cap, width),
        "relay": rows_b(chips * cap, width),
        "recv": rows_b(chips * cap, width),
        "back_relay": rows_b(chips * cap, width),
        "back": rows_b(chips * cap, width),
        "turned": rows_f(width, positions),
        "embedded": rows_f(positions, width),
        "x_all": rows_b(total, width),
        "g_all": rows_b(total, width),
        "gate": rows_b(total, cols),
        "value": rows_b(total, cols),
        "query": rows_b(total, cols),
        "keyrow": rows_b(total, cols),
        "slope": rows_b(total, 4 * cols),
        "grad_gated": pltpu.VMEM((2, block, cols), F32),
        "attended": pltpu.VMEM((2, block, cols), F32),
        "stat_send": rows_f(total, 128),
        "stat_recv": rows_f(total, 128),
        "soft": pairs,
        "soft_slope": pairs,
        "grad_att": rows_b(block, cols),
        "grad_q": rows_f(block, cols),
        "grad_k": rows_f(total, cols),
        "grad_v": rows_f(total, cols),
        "gated_own": rows_b(positions, cols),
        "gated_send": rows_b(positions, cols),
        "gated_recv": rows_b(positions, cols),
        "gx_own": rows_f(positions, width),
        "gx_send": rows_f(positions, width),
        "gx_recv": rows_f(positions, width),
        "grads": rows_b(positions, width),
        "half_send": rows_b(table_rows // 2, width),
        "load_sem": sems((9,)),
        "store_sem": sems((2,)),
        "core_out_sem": sems((copies,)),
        "core_in_sem": sems((copies,)),
    }
    for way in ("ask", "give"):
        scratch[way + "_z_out"], scratch[way + "_z_in"] = sems((chips,)), sems((chips,))
        scratch[way + "_out"], scratch[way + "_in"] = sems((side * side,)), sems((side * side,))
    results = pl.pallas_call(
        functools.partial(kernel, side, cap, block),
        out_shape=(
            jax.ShapeDtypeStruct((positions, width), BF16),
            jax.ShapeDtypeStruct((table_rows // 2, width), F32),
            jax.ShapeDtypeStruct((table_rows // 2, width), BF16),
        ),
        in_specs=[anywhere] * 3 + [pl.BlockSpec(memory_space=pltpu.SMEM)] + [anywhere] * 3,
        out_specs=(anywhere,) * 3,
        scratch_shapes=list(scratch.values()),
        compiler_params=pltpu.CompilerParams(
            collective_id=0, has_side_effects=True, vmem_limit_bytes=63 << 20
        ),
        name="hstu",
    )(item_table, serve_rows, slots, lengths, w_proj, w_out, grad_out[0])
    layer_out, grad_table = finish(*results)
    return (layer_out[None], grad_table)


def solution(mesh):
    placed = (
        P("table", None),
        P("table", "ctx"),
        P("table", "ctx", None),
        P("table"),
        P(),
        P(),
        P("table", "ctx", None),
    )
    side = round(mesh.shape["table"] ** (1 / 3))
    return jax.shard_map(
        functools.partial(on_device, side),
        mesh=mesh,
        in_specs=placed,
        out_specs=(P("table", "ctx", None), P(("table", "ctx"), None)),
        check_vma=False,
    )
```

```python
import functools

import jax
import jax.numpy as jnp
from jax import lax
from jax.experimental import pallas as pl
from jax.experimental.pallas import tpu as pltpu
from jax.sharding import PartitionSpec as P

HEAD = 128
EPS = 1e-05
SCALE = HEAD**-0.5
MESH = pl.DeviceIdType.MESH
F32 = jnp.float32
BF16 = jnp.bfloat16
NN = (((1,), (0,)), ((), ()))
NT = (((1,), (1,)), ((), ()))
TN = (((0,), (0,)), ((), ()))


def dot(a, b, form=NN):
    return lax.dot_general(a, b, form, preferred_element_type=F32)


def iota(shape, dim):
    return lax.broadcasted_iota(jnp.int32, shape, dim)


def place(step, lane, side, sign):
    me = lax.axis_index("table")
    z, y, x = lax.div(me, side * side), lax.rem(lax.div(me, side), side), lax.rem(me, side)
    far = lax.div(step, side) if isinstance(step, jax.Array) else step // side
    if sign > 0:
        z, y, x = z + lane, y + far + lane, x + step + lane
    else:
        z, y, x = z - lane + side, y - far - lane + 2 * side, x - step - lane + (side + 1) * side
    return (lax.rem(z, side) * side + lax.rem(y, side)) * side + lax.rem(x, side)


def greet_all(side):
    barrier = pltpu.get_barrier_semaphore()
    core = lax.axis_index("ctx")

    def greet(step, lane):
        pl.semaphore_signal(
            barrier, inc=1, device_id=(place(step, lane, side, 1), core), device_id_type=MESH
        )

    for lane in range(1, side):
        greet(0, lane)

    @pl.loop(1, side * side)
    def _(step):
        for lane in range(side):
            greet(step, lane)


def exchange(side, cap, send, recv, send_sem, recv_sem, step, lane):
    row = pl.multiple_of((step * side + lane) * cap, cap)
    return pltpu.make_async_remote_copy(
        src_ref=send.at[pl.ds(row, cap)],
        dst_ref=recv.at[pl.ds(row, cap)],
        send_sem=send_sem.at[step * side + lane],
        recv_sem=recv_sem.at[step * side + lane],
        device_id=(place(step, lane, side, 1), lax.axis_index("ctx")),
        device_id_type=MESH,
    )


def for_steps(side, body):
    body(0, 1)

    @pl.loop(1, side * side)
    def _(step):
        body(step, 0)


def multi_hot(slots_ref, base, rows, start, columns):
    row = iota((rows, columns), 0) + base
    total = jnp.zeros((rows, columns), F32)
    for feature in range(slots_ref.shape[0]):
        total = total + jnp.where(slots_ref[feature : feature + 1, start : start + columns] == row, 1.0, 0.0)
    return total.astype(BF16)


def kernel(
    side, cap, block,
    table_in, serve_in, slots_in, lengths, w_proj_in, w_out_in, cotangent_in,
    layer_out, own_half, their_half,
    serve, slots, weights_own, w_out, cotangent, picked, send, recv, back, turned, embedded,
    x_all, g_all, gate, value, query, keyrow, slope, grad_gated, attended, stat_send, stat_recv,
    soft, soft_slope, grad_att, grad_q, grad_k, grad_v, gated_own, gated_send, gated_recv,
    gx_own, gx_send, gx_recv, grads, half_send,
    load_sem, store_sem, out_sem, in_sem, back_out_sem, back_in_sem, core_out_sem, core_in_sem,
):
    table, core = lax.axis_index("table"), lax.axis_index("ctx")
    other = (table, 1 - core)
    barrier = pltpu.get_barrier_semaphore()
    steps = side * side
    lanes = side * cap
    table_rows, width = grad_k.shape
    positions = slots.shape[1]
    cols = value.shape[1]
    heads = cols // HEAD
    own_blocks = positions // block
    blocks = 2 * own_blocks
    first = core * own_blocks
    length = lengths[0]
    own_cols = pl.multiple_of(core * cols, cols)
    their_cols = pl.multiple_of((1 - core) * cols, cols)

    loads = [(serve_in, serve), (table_in, grad_k), (slots_in, slots), (cotangent_in, cotangent)]
    for part in range(4):
        here = pl.multiple_of(part * 2 * cols + core * cols, cols)
        loads.append((w_proj_in.at[:, pl.ds(here, cols)], weights_own.at[part]))
    loads.append((w_out_in, w_out))
    loads = [
        pltpu.make_async_copy(src, dst, load_sem.at[number])
        for number, (src, dst) in enumerate(loads)
    ]
    for load in loads[:2]:
        load.start()
    greet_all(side)
    pl.semaphore_signal(barrier, inc=1, device_id=other, device_id_type=MESH)
    for load in loads[2:]:
        load.start()

    rounded = keyrow
    loads[0].wait()
    loads[1].wait()
    rounded[...] = grad_k[...].astype(BF16)
    square = iota((cap, cap), 0) == iota((cap, cap), 1)
    columns = iota((cap, table_rows), 1)

    def pick(step):
        for lane in range(side):
            ids = serve[pl.ds(place(step, lane, side, 1), 1), :]
            ids = jnp.sum(jnp.where(square, ids.astype(F32), 0.0), axis=1, keepdims=True)
            one_hot = jnp.where(ids.astype(jnp.int32) == columns, 1.0, 0.0)
            picked[lane * cap : (lane + 1) * cap, :] = one_hot.astype(BF16)
        row = pl.multiple_of(step * lanes, lanes)
        send[pl.ds(row, lanes), :] = dot(picked[...], rounded[...]).astype(BF16)

    ask = functools.partial(exchange, side, cap, send, recv, out_sem, in_sem)

    def start_ask(step, first_lane):
        for lane in range(first_lane, side):
            ask(step, lane).start()

    early = 2
    for step in range(early):
        pick(step)
    pl.semaphore_wait(barrier, side**3)
    for step in range(early):
        start_ask(step, 1 if step == 0 else 0)
    recv[0:cap, :] = send[0:cap, :]

    @pl.loop(early, steps)
    def _(step):
        pick(step)
        start_ask(step, 0)

    for load in loads[2:]:
        load.wait()

    def rows_of(index):
        if isinstance(index, int):
            return pl.ds(index * block, block)
        return pl.ds(pl.multiple_of(index * block, block), block)

    def valid(index, height):
        return iota((height, 1), 0) + index * block < length

    def copy_over(src, dst, number):
        return pltpu.make_async_remote_copy(
            src_ref=src,
            dst_ref=dst,
            send_sem=core_out_sem.at[number],
            recv_sem=core_in_sem.at[number],
            device_id=other,
            device_id_type=MESH,
        )

    at_g, at_x = 0, own_blocks
    at_stat = 2 * own_blocks
    at_gated = at_stat + blocks
    at_gx = at_gated + own_blocks
    at_half = at_gx + own_blocks

    def send_x(index):
        here = rows_of(first + index)
        return copy_over(x_all.at[here], x_all.at[here], at_x + index)

    def send_g(index):
        here = rows_of(first + index)
        return copy_over(g_all.at[here], g_all.at[here], at_g + index)

    for index in range(own_blocks):
        rows_g = cotangent[rows_of(index), :]
        g_all[rows_of(first + index), :] = jnp.where(
            valid(first + index, block), rows_g, jnp.zeros_like(rows_g)
        )
        send_g(index).start()
    grad_k[...] = jnp.zeros_like(grad_k)
    grad_v[...] = jnp.zeros_like(grad_v)
    turned[...] = jnp.zeros_like(turned)

    def hot_rows(index, row, count):
        return pl.ds(pl.multiple_of(index * steps * lanes + row, cap), count)

    @pl.loop(0, steps)
    def _(step):
        for lane in range(side):
            base = place(step, lane, side, -1) * cap
            row = pl.multiple_of((step * side + lane) * cap, cap)
            for index in range(own_blocks):
                soft[hot_rows(index, row, cap), :] = multi_hot(slots, base, cap, index * block, block)

    for index in range(own_blocks):
        send_g(index).wait_recv()

    def take(step, first_lane):
        for lane in range(first_lane, side):
            ask(step, lane).wait_recv()
        row = pl.multiple_of(step * lanes, lanes)
        for index in range(own_blocks):
            turned[:, index * block : (index + 1) * block] += dot(
                recv[pl.ds(row, lanes), :], soft[hot_rows(index, row, lanes), :], TN
            )

    for_steps(side, take)
    embedded[...] = turned[...].T

    def normalize(index):
        rows_x = embedded[rows_of(index), :]
        centred = rows_x - jnp.mean(rows_x, axis=-1, keepdims=True)
        inverse = lax.rsqrt(jnp.mean(centred * centred, axis=-1, keepdims=True) + EPS)
        return centred * inverse, inverse

    for index in range(own_blocks):
        x_all[rows_of(first + index), :] = normalize(index)[0].astype(BF16)
        send_x(index).start()

    def project(index):
        here = rows_of(index)
        rows_x = x_all[here, :]
        for part, ref in enumerate((gate, value, query, keyrow)):
            h = dot(rows_x, weights_own[part]) * 0.5
            th = jnp.tanh(h)
            up = 1.0 + th
            act = h * up
            slope[here, part * cols : (part + 1) * cols] = (
                0.5 * (up + act * (1.0 - th))
            ).astype(BF16)
            act = act.astype(BF16)
            if part == 1:
                act = jnp.where(valid(index, block), act, jnp.zeros_like(act))
            ref[here, :] = act

    @pl.loop(0, own_blocks)
    def _(index):
        project(first + index)

    @pl.loop(0, own_blocks)
    def _(index):
        send_x(index).wait_recv()
        project((1 - core) * own_blocks + index)

    def head(number):
        return slice(number * HEAD, (number + 1) * HEAD)

    def pair_ref(ref, i, number, j):
        row = (((i % 2) * heads + number) * blocks + j) * block
        return ref.at[pl.ds(row, block)]

    def forward_pair(i, j, masked):
        for number in range(heads):
            h = dot(query[rows_of(i), head(number)], keyrow[rows_of(j), head(number)], NT)
            h = h * (0.5 * SCALE)
            th = jnp.tanh(h)
            up = 1.0 + th
            act = h * up
            twice = up + act * (1.0 - th)
            if masked:
                allowed = iota((block, block), 1) <= iota((block, block), 0)
                act = jnp.where(allowed, act, 0.0)
                twice = jnp.where(allowed, twice, 0.0)
            act = act.astype(BF16)
            pair_ref(soft, i, number, j)[...] = act
            pair_ref(soft_slope, i, number, j)[...] = twice.astype(BF16)
            added = dot(act, value[rows_of(j), head(number)])
            if masked:
                attended[i % 2, :, head(number)] = added
            else:
                attended[i % 2, :, head(number)] += added

    def send_stat(i):
        return copy_over(stat_send.at[rows_of(i)], stat_recv.at[rows_of(i)], at_stat + i)

    def forward(i):
        forward_pair(i, i, True)
        here = rows_of(i)
        grad_gated[i % 2] = dot(g_all[here, :], w_out[pl.ds(own_cols, cols), :], NT)

        for j in range(i):
            forward_pair(i, j, False)

        att = attended[i % 2]
        t = grad_gated[i % 2] * gate[here, :].astype(F32)
        lane = iota((block, 128), 1)
        sums = jnp.zeros((block, 128), F32)
        for number, term in enumerate((att, att * att, t, t * att)):
            sums = jnp.where(lane == number, jnp.sum(term, axis=1, keepdims=True), sums)
        stat_send[here, :] = sums
        send_stat(i).start()

    def is_own(i):
        return (i // own_blocks) == core

    def send_gated(index):
        here = rows_of(index)
        return copy_over(gated_send.at[here], gated_recv.at[here], at_gated + index)

    def send_gx(index):
        here = rows_of(index)
        return copy_over(gx_send.at[here], gx_recv.at[here], at_gx + index)

    def combine(i):
        here = rows_of(i)
        send_stat(i).wait_recv()
        mean = (stat_send[here, :] + stat_recv[here, :]) * (1.0 / (2 * cols))
        middle = mean[:, 0:1]
        inverse = lax.rsqrt(mean[:, 1:2] - middle * middle + EPS)
        mean_t = mean[:, 2:3]
        mean_tn = (mean[:, 3:4] - middle * mean_t) * inverse
        gates = gate[here, :].astype(F32)
        grad_rows = grad_gated[i % 2]
        normed = (attended[i % 2] - middle) * inverse
        gated = (normed * gates).astype(BF16)
        grad_att[...] = ((grad_rows * gates - mean_t - normed * mean_tn) * inverse).astype(BF16)
        grad_gated[i % 2] = grad_rows * normed
        local = rows_of(i % own_blocks)

        @pl.when(is_own(i))
        def _():
            gated_own[local, :] = gated

        @pl.when(jnp.logical_not(is_own(i)))
        def _():
            gated_send[local, :] = gated
            send_gated(i % own_blocks).start()

    def backward_pair(i, j):
        for number in range(heads):
            at = head(number)
            grad_rows = grad_att[:, at]
            grad_p = dot(grad_rows, value[rows_of(j), at], NT)
            twice = pair_ref(soft_slope, i, number, j)[...]
            grad_s = (grad_p * twice.astype(F32)).astype(BF16)
            grad_v[rows_of(j), at] += dot(pair_ref(soft, i, number, j)[...], grad_rows, TN)
            grad_k[rows_of(j), at] += dot(grad_s, query[rows_of(i), at], TN)
            grad_q[:, at] += dot(grad_s, keyrow[rows_of(j), at])

    def backward(i):
        combine(i)
        grad_q[...] = jnp.zeros_like(grad_q)

        for j in range(i + 1):
            backward_pair(i, j)

        here = rows_of(i)
        total = jnp.zeros((block, width), F32)
        for part in range(4):
            if part == 0:
                term = grad_gated[i % 2]
            elif part == 1:
                term = jnp.where(valid(i, block), grad_v[here, :], 0.0)
            elif part == 2:
                term = grad_q[...] * (0.5 * SCALE)
            else:
                term = grad_k[here, :] * (0.5 * SCALE)
            slopes = slope[here, part * cols : (part + 1) * cols].astype(F32)
            total = total + dot((term * slopes).astype(BF16), weights_own[part], NT)
        local = rows_of(i % own_blocks)

        @pl.when(is_own(i))
        def _():
            gx_own[local, :] = total

        @pl.when(jnp.logical_not(is_own(i)))
        def _():
            gx_send[local, :] = total.astype(BF16)
            send_gx(i % own_blocks).start()

    forward(blocks - 1)

    for step in range(blocks - 1):
        forward(blocks - 2 - step)
        backward(blocks - 1 - step)

    backward(0)

    def mix(index):
        here = rows_of(index)
        send_gated(index).wait_recv()
        mixed = dot(gated_own[here, :], w_out[pl.ds(own_cols, cols), :]) + dot(
            gated_recv[here, :], w_out[pl.ds(their_cols, cols), :]
        )
        cotangent[here, :] = jnp.where(
            valid(first + index, block), embedded[here, :] + mixed, 0.0
        ).astype(BF16)

    for index in reversed(range(own_blocks)):
        here = rows_of(index)
        normal_x, inverse = normalize(index)
        send_gx(index).wait_recv()
        grad_x = gx_own[here, :] + gx_recv[here, :].astype(F32)
        middle = jnp.mean(grad_x, axis=-1, keepdims=True)
        along = jnp.mean(grad_x * normal_x, axis=-1, keepdims=True)
        masked = g_all[rows_of(first + index), :].astype(F32)
        grads[here, :] = (masked + (grad_x - middle - normal_x * along) * inverse).astype(BF16)

    def sent(step, first_lane):
        for lane in range(first_lane, side):
            ask(step, lane).wait_send()

    for_steps(side, sent)
    give = functools.partial(exchange, side, cap, send, back, back_out_sem, back_in_sem)

    def sums_back(step):
        for lane in range(side):
            base = place(step, lane, side, 1) * cap
            picked[lane * cap : (lane + 1) * cap, 0:positions] = multi_hot(
                slots, base, cap, 0, positions
            )
        row = pl.multiple_of(step * lanes, lanes)
        send[pl.ds(row, lanes), :] = dot(picked[:, 0:positions], grads[...]).astype(BF16)

    def start_give(step, first_lane):
        for lane in range(first_lane, side):
            give(step, lane).start()

    sums_back(0)
    start_give(0, 1)
    back[0:cap, :] = send[0:cap, :]

    @pl.loop(1, steps)
    def _(step):
        sums_back(step)
        start_give(step, 0)

    for index in range(own_blocks):
        mix(index)
    store = pltpu.make_async_copy(cotangent, layer_out, store_sem.at[0])
    store.start()
    total = grad_k
    total[...] = jnp.zeros_like(total)

    def add(step, first_lane):
        ids = [serve[pl.ds(place(step, lane, side, -1), 1), :] for lane in range(side)]
        one_hot = jnp.where(
            jnp.concatenate(ids, axis=1) == iota((table_rows, lanes), 0), 1.0, 0.0
        ).astype(BF16)
        for lane in range(first_lane, side):
            give(step, lane).wait_recv()
        row = pl.multiple_of(step * lanes, lanes)
        total[...] += dot(one_hot, back[pl.ds(row, lanes), :])

    for_steps(side, add)
    half = table_rows // 2
    mine = pl.ds(pl.multiple_of(core * half, half), half)
    theirs = pl.ds(pl.multiple_of((1 - core) * half, half), half)
    half_send[...] = total[theirs, :].astype(BF16)
    swap = copy_over(half_send, their_half, at_half)
    swap.start()
    last = pltpu.make_async_copy(total.at[mine], own_half, store_sem.at[1])
    last.start()

    def given(step, first_lane):
        for lane in range(first_lane, side):
            give(step, lane).wait_send()

    for_steps(side, given)
    for index in range(own_blocks):
        send_x(index).wait_send()
        send_g(index).wait_send()
        send_gated(index).wait_send()
        send_gx(index).wait_send()

    @pl.loop(0, blocks)
    def _(i):
        send_stat(i).wait_send()

    store.wait()
    last.wait()
    swap.wait()


def finish_kernel(rows, own, their, rows_out, total_out, held, mine, theirs, load_sem, store_sem):
    half = own.shape[0] // 2
    loads = []
    for part in range(2):
        here = slice(part * half, (part + 1) * half)
        for number, (src, dst) in enumerate(((own, mine), (their, theirs))):
            loads.append(
                pltpu.make_async_copy(src.at[here], dst.at[here], load_sem.at[2 * part + number])
            )
    loads.append(pltpu.make_async_copy(rows, held, load_sem.at[4]))
    for load in loads:
        load.start()
    stores = []
    for part in range(2):
        here = slice(part * half, (part + 1) * half)
        loads[2 * part].wait()
        loads[2 * part + 1].wait()
        mine[here, :] = mine[here, :] + theirs[here, :].astype(F32)
        stores.append(pltpu.make_async_copy(mine.at[here], total_out.at[here], store_sem.at[part]))
        stores[-1].start()
    loads[4].wait()
    stores.append(pltpu.make_async_copy(held, rows_out, store_sem.at[2]))
    stores[-1].start()
    for store in stores:
        store.wait()


def finish(rows, own, their):
    anywhere = pl.BlockSpec(memory_space=pl.ANY)
    return pl.pallas_call(
        finish_kernel,
        out_shape=(
            jax.ShapeDtypeStruct(rows.shape, rows.dtype),
            jax.ShapeDtypeStruct(own.shape, own.dtype),
        ),
        in_specs=[anywhere] * 3,
        out_specs=(anywhere, anywhere),
        scratch_shapes=[
            pltpu.VMEM(rows.shape, rows.dtype),
            pltpu.VMEM(own.shape, own.dtype),
            pltpu.VMEM(their.shape, their.dtype),
            pltpu.SemaphoreType.DMA((5,)),
            pltpu.SemaphoreType.DMA((3,)),
        ],
        compiler_params=pltpu.CompilerParams(vmem_limit_bytes=63 << 20),
        name="finish",
    )(rows, own, their)


def on_device(side, item_table, serve_rows, token_slots, lengths, w_proj, w_out, grad_out):
    slots = token_slots[0].T
    cap = serve_rows.shape[1]
    chips = side**3
    table_rows, width = item_table.shape
    positions = slots.shape[1]
    block = min(512, positions)
    total = 2 * positions
    cols = w_out.shape[0] // 2
    heads = cols // HEAD
    own_blocks = positions // block
    blocks = 2 * own_blocks
    copies = 4 * own_blocks + blocks + 1
    anywhere = pl.BlockSpec(memory_space=pl.ANY)
    sems = pltpu.SemaphoreType.DMA

    def rows_b(rows, columns):
        return pltpu.VMEM((rows, columns), BF16)

    def rows_f(rows, columns):
        return pltpu.VMEM((rows, columns), F32)

    pairs = rows_b(2 * heads * blocks * block, block)
    scratch = {
        "serve": pltpu.VMEM(serve_rows.shape, jnp.int32),
        "slots": pltpu.VMEM(slots.shape, jnp.int32),
        "weights_own": pltpu.VMEM((4, width, cols), BF16),
        "w_out": pltpu.VMEM(w_out.shape, BF16),
        "cotangent": rows_b(positions, width),
        "picked": rows_b(side * cap, table_rows),
        "send": rows_b(chips * cap, width),
        "recv": rows_b(chips * cap, width),
        "back": rows_b(chips * cap, width),
        "turned": rows_f(width, positions),
        "embedded": rows_f(positions, width),
        "x_all": rows_b(total, width),
        "g_all": rows_b(total, width),
        "gate": rows_b(total, cols),
        "value": rows_b(total, cols),
        "query": rows_b(total, cols),
        "keyrow": rows_b(total, cols),
        "slope": rows_b(total, 4 * cols),
        "grad_gated": pltpu.VMEM((2, block, cols), F32),
        "attended": pltpu.VMEM((2, block, cols), F32),
        "stat_send": rows_f(total, 128),
        "stat_recv": rows_f(total, 128),
        "soft": pairs,
        "soft_slope": pairs,
        "grad_att": rows_b(block, cols),
        "grad_q": rows_f(block, cols),
        "grad_k": rows_f(total, cols),
        "grad_v": rows_f(total, cols),
        "gated_own": rows_b(positions, cols),
        "gated_send": rows_b(positions, cols),
        "gated_recv": rows_b(positions, cols),
        "gx_own": rows_f(positions, width),
        "gx_send": rows_b(positions, width),
        "gx_recv": rows_b(positions, width),
        "grads": rows_b(positions, width),
        "half_send": rows_b(table_rows // 2, width),
        "load_sem": sems((9,)),
        "store_sem": sems((2,)),
        "out_sem": sems((chips,)),
        "in_sem": sems((chips,)),
        "back_out_sem": sems((chips,)),
        "back_in_sem": sems((chips,)),
        "core_out_sem": sems((copies,)),
        "core_in_sem": sems((copies,)),
    }
    results = pl.pallas_call(
        functools.partial(kernel, side, cap, block),
        out_shape=(
            jax.ShapeDtypeStruct((positions, width), BF16),
            jax.ShapeDtypeStruct((table_rows // 2, width), F32),
            jax.ShapeDtypeStruct((table_rows // 2, width), BF16),
        ),
        in_specs=[anywhere] * 3 + [pl.BlockSpec(memory_space=pltpu.SMEM)] + [anywhere] * 3,
        out_specs=(anywhere,) * 3,
        scratch_shapes=list(scratch.values()),
        compiler_params=pltpu.CompilerParams(
            collective_id=0, has_side_effects=True, vmem_limit_bytes=63 << 20
        ),
        name="hstu",
    )(item_table, serve_rows, slots, lengths, w_proj, w_out, grad_out[0])
    layer_out, grad_table = finish(*results)
    return (layer_out[None], grad_table)


def solution(mesh):
    placed = (
        P("table", None),
        P("table", "ctx"),
        P("table", "ctx", None),
        P("table"),
        P(),
        P(),
        P("table", "ctx", None),
    )
    side = round(mesh.shape["table"] ** (1 / 3))
    return jax.shard_map(
        functools.partial(on_device, side),
        mesh=mesh,
        in_specs=placed,
        out_specs=(P("table", "ctx", None), P(("table", "ctx"), None)),
        check_vma=False,
    )
```

```python
import functools

import jax
import jax.numpy as jnp
from jax import lax
from jax.experimental import pallas as pl
from jax.experimental.pallas import tpu as pltpu
from jax.sharding import PartitionSpec as P

HEAD = 128
EPS = 1e-05
SCALE = HEAD**-0.5
MESH = pl.DeviceIdType.MESH
F32 = jnp.float32
BF16 = jnp.bfloat16
NN = (((1,), (0,)), ((), ()))
NT = (((1,), (1,)), ((), ()))
TN = (((0,), (0,)), ((), ()))


def dot(a, b, form=NN):
    return lax.dot_general(a, b, form, preferred_element_type=F32)


def iota(shape, dim):
    return lax.broadcasted_iota(jnp.int32, shape, dim)


def place(step, lane, side, sign):
    me = lax.axis_index("table")
    z, y, x = lax.div(me, side * side), lax.rem(lax.div(me, side), side), lax.rem(me, side)
    far = lax.div(step, side) if isinstance(step, jax.Array) else step // side
    if sign > 0:
        z, y, x = z + lane, y + far + lane, x + step + lane
    else:
        z, y, x = z - lane + side, y - far - lane + 2 * side, x - step - lane + (side + 1) * side
    return (lax.rem(z, side) * side + lax.rem(y, side)) * side + lax.rem(x, side)


def greet_all(side):
    barrier = pltpu.get_barrier_semaphore()
    core = lax.axis_index("ctx")

    def greet(step, lane):
        pl.semaphore_signal(
            barrier, inc=1, device_id=(place(step, lane, side, 1), core), device_id_type=MESH
        )

    for lane in range(1, side):
        greet(0, lane)

    @pl.loop(1, side * side)
    def _(step):
        for lane in range(side):
            greet(step, lane)


def exchange(side, cap, send, recv, send_sem, recv_sem, step, lane):
    row = pl.multiple_of((step * side + lane) * cap, cap)
    return pltpu.make_async_remote_copy(
        src_ref=send.at[pl.ds(row, cap)],
        dst_ref=recv.at[pl.ds(row, cap)],
        send_sem=send_sem.at[step * side + lane],
        recv_sem=recv_sem.at[step * side + lane],
        device_id=(place(step, lane, side, 1), lax.axis_index("ctx")),
        device_id_type=MESH,
    )


def for_steps(side, body):
    body(0, 1)

    @pl.loop(1, side * side)
    def _(step):
        body(step, 0)


def multi_hot(slots_ref, base, rows, start, columns):
    row = iota((rows, columns), 0) + base
    total = jnp.zeros((rows, columns), F32)
    for feature in range(slots_ref.shape[0]):
        total = total + jnp.where(slots_ref[feature : feature + 1, start : start + columns] == row, 1.0, 0.0)
    return total.astype(BF16)


def kernel(
    side, cap, block,
    table_in, serve_in, slots_in, lengths, w_proj_in, w_out_in, cotangent_in,
    layer_out, own_half, their_half,
    serve, slots, weights_own, w_out, cotangent, picked, send, recv, back, turned, embedded,
    x_all, g_all, gate, value, query, keyrow, slope, grad_gated, attended, stat_send, stat_recv,
    soft, soft_slope, grad_att, grad_q, grad_k, grad_v, gated_own, gated_send, gated_recv,
    gx_own, gx_send, gx_recv, grads, half_send,
    load_sem, store_sem, out_sem, in_sem, back_out_sem, back_in_sem, core_out_sem, core_in_sem,
):
    table, core = lax.axis_index("table"), lax.axis_index("ctx")
    other = (table, 1 - core)
    barrier = pltpu.get_barrier_semaphore()
    steps = side * side
    lanes = side * cap
    table_rows, width = grad_k.shape
    positions = slots.shape[1]
    cols = value.shape[1]
    heads = cols // HEAD
    own_blocks = positions // block
    blocks = 2 * own_blocks
    first = core * own_blocks
    length = lengths[0]
    own_cols = pl.multiple_of(core * cols, cols)
    their_cols = pl.multiple_of((1 - core) * cols, cols)

    loads = [(serve_in, serve), (table_in, grad_k), (slots_in, slots), (cotangent_in, cotangent)]
    for part in range(4):
        here = pl.multiple_of(part * 2 * cols + core * cols, cols)
        loads.append((w_proj_in.at[:, pl.ds(here, cols)], weights_own.at[part]))
    loads.append((w_out_in, w_out))
    loads = [
        pltpu.make_async_copy(src, dst, load_sem.at[number])
        for number, (src, dst) in enumerate(loads)
    ]
    for load in loads[:2]:
        load.start()
    greet_all(side)
    pl.semaphore_signal(barrier, inc=1, device_id=other, device_id_type=MESH)
    for load in loads[2:]:
        load.start()

    rounded = keyrow
    loads[0].wait()
    loads[1].wait()
    rounded[...] = grad_k[...].astype(BF16)
    square = iota((cap, cap), 0) == iota((cap, cap), 1)
    columns = iota((cap, table_rows), 1)

    def pick(step):
        for lane in range(side):
            ids = serve[pl.ds(place(step, lane, side, 1), 1), :]
            ids = jnp.sum(jnp.where(square, ids.astype(F32), 0.0), axis=1, keepdims=True)
            one_hot = jnp.where(ids.astype(jnp.int32) == columns, 1.0, 0.0)
            picked[lane * cap : (lane + 1) * cap, :] = one_hot.astype(BF16)
        row = pl.multiple_of(step * lanes, lanes)
        send[pl.ds(row, lanes), :] = dot(picked[...], rounded[...]).astype(BF16)

    ask = functools.partial(exchange, side, cap, send, recv, out_sem, in_sem)

    def start_ask(step, first_lane):
        for lane in range(first_lane, side):
            ask(step, lane).start()

    early = 2
    for step in range(early):
        pick(step)
    pl.semaphore_wait(barrier, side**3)
    for step in range(early):
        start_ask(step, 1 if step == 0 else 0)
    recv[0:cap, :] = send[0:cap, :]

    @pl.loop(early, steps)
    def _(step):
        pick(step)
        start_ask(step, 0)

    for load in loads[2:]:
        load.wait()

    def rows_of(index):
        if isinstance(index, int):
            return pl.ds(index * block, block)
        return pl.ds(pl.multiple_of(index * block, block), block)

    def valid(index, height):
        return iota((height, 1), 0) + index * block < length

    def copy_over(src, dst, number):
        return pltpu.make_async_remote_copy(
            src_ref=src,
            dst_ref=dst,
            send_sem=core_out_sem.at[number],
            recv_sem=core_in_sem.at[number],
            device_id=other,
            device_id_type=MESH,
        )

    at_g, at_x = 0, own_blocks
    at_stat = 2 * own_blocks
    at_gated = at_stat + blocks
    at_gx = at_gated + own_blocks
    at_half = at_gx + own_blocks

    def send_x(index):
        here = rows_of(first + index)
        return copy_over(x_all.at[here], x_all.at[here], at_x + index)

    def send_g(index):
        here = rows_of(first + index)
        return copy_over(g_all.at[here], g_all.at[here], at_g + index)

    for index in range(own_blocks):
        rows_g = cotangent[rows_of(index), :]
        g_all[rows_of(first + index), :] = jnp.where(
            valid(first + index, block), rows_g, jnp.zeros_like(rows_g)
        )
        send_g(index).start()
    grad_k[...] = jnp.zeros_like(grad_k)
    grad_v[...] = jnp.zeros_like(grad_v)
    turned[...] = jnp.zeros_like(turned)

    def hot_rows(index, row, count):
        return pl.ds(pl.multiple_of(index * steps * lanes + row, cap), count)

    @pl.loop(0, steps)
    def _(step):
        for lane in range(side):
            base = place(step, lane, side, -1) * cap
            row = pl.multiple_of((step * side + lane) * cap, cap)
            for index in range(own_blocks):
                soft[hot_rows(index, row, cap), :] = multi_hot(slots, base, cap, index * block, block)

    for index in range(own_blocks):
        send_g(index).wait_recv()

    def take(step, first_lane):
        for lane in range(first_lane, side):
            ask(step, lane).wait_recv()
        row = pl.multiple_of(step * lanes, lanes)
        for index in range(own_blocks):
            turned[:, index * block : (index + 1) * block] += dot(
                recv[pl.ds(row, lanes), :], soft[hot_rows(index, row, lanes), :], TN
            )

    for_steps(side, take)
    embedded[...] = turned[...].T

    def sent(step, first_lane):
        for lane in range(first_lane, side):
            ask(step, lane).wait_send()

    for_steps(side, sent)

    def normalize(index):
        rows_x = embedded[rows_of(index), :]
        centred = rows_x - jnp.mean(rows_x, axis=-1, keepdims=True)
        inverse = lax.rsqrt(jnp.mean(centred * centred, axis=-1, keepdims=True) + EPS)
        return centred * inverse, inverse

    for index in range(own_blocks):
        x_all[rows_of(first + index), :] = normalize(index)[0].astype(BF16)
        send_x(index).start()

    def project(index):
        here = rows_of(index)
        rows_x = x_all[here, :]
        for part, ref in enumerate((gate, value, query, keyrow)):
            h = dot(rows_x, weights_own[part]) * 0.5
            th = jnp.tanh(h)
            up = 1.0 + th
            act = h * up
            slope[here, part * cols : (part + 1) * cols] = (
                0.5 * (up + act * (1.0 - th))
            ).astype(BF16)
            act = act.astype(BF16)
            if part == 1:
                act = jnp.where(valid(index, block), act, jnp.zeros_like(act))
            ref[here, :] = act

    @pl.loop(0, own_blocks)
    def _(index):
        project(first + index)

    @pl.loop(0, own_blocks)
    def _(index):
        send_x(index).wait_recv()
        project((1 - core) * own_blocks + index)

    def head(number):
        return slice(number * HEAD, (number + 1) * HEAD)

    def pair_ref(ref, i, number, j):
        row = (((i % 2) * heads + number) * blocks + j) * block
        return ref.at[pl.ds(row, block)]

    def forward_pair(i, j, masked):
        for number in range(heads):
            h = dot(query[rows_of(i), head(number)], keyrow[rows_of(j), head(number)], NT)
            h = h * (0.5 * SCALE)
            th = jnp.tanh(h)
            up = 1.0 + th
            act = h * up
            twice = up + act * (1.0 - th)
            if masked:
                allowed = iota((block, block), 1) <= iota((block, block), 0)
                act = jnp.where(allowed, act, 0.0)
                twice = jnp.where(allowed, twice, 0.0)
            act = act.astype(BF16)
            pair_ref(soft, i, number, j)[...] = act
            pair_ref(soft_slope, i, number, j)[...] = twice.astype(BF16)
            added = dot(act, value[rows_of(j), head(number)])
            if masked:
                attended[i % 2, :, head(number)] = added
            else:
                attended[i % 2, :, head(number)] += added

    def send_stat(i):
        return copy_over(stat_send.at[rows_of(i)], stat_recv.at[rows_of(i)], at_stat + i)

    def forward(i):
        forward_pair(i, i, True)
        here = rows_of(i)
        grad_gated[i % 2] = dot(g_all[here, :], w_out[pl.ds(own_cols, cols), :], NT)

        for j in range(i):
            forward_pair(i, j, False)

        att = attended[i % 2]
        t = grad_gated[i % 2] * gate[here, :].astype(F32)
        lane = iota((block, 128), 1)
        sums = jnp.zeros((block, 128), F32)
        for number, term in enumerate((att, att * att, t, t * att)):
            sums = jnp.where(lane == number, jnp.sum(term, axis=1, keepdims=True), sums)
        stat_send[here, :] = sums
        send_stat(i).start()

    def is_own(i):
        return (i // own_blocks) == core

    def send_gated(index):
        here = rows_of(index)
        return copy_over(gated_send.at[here], gated_recv.at[here], at_gated + index)

    def send_gx(index):
        here = rows_of(index)
        return copy_over(gx_send.at[here], gx_recv.at[here], at_gx + index)

    def combine(i):
        here = rows_of(i)
        send_stat(i).wait_recv()
        mean = (stat_send[here, :] + stat_recv[here, :]) * (1.0 / (2 * cols))
        middle = mean[:, 0:1]
        inverse = lax.rsqrt(mean[:, 1:2] - middle * middle + EPS)
        mean_t = mean[:, 2:3]
        mean_tn = (mean[:, 3:4] - middle * mean_t) * inverse
        gates = gate[here, :].astype(F32)
        grad_rows = grad_gated[i % 2]
        normed = (attended[i % 2] - middle) * inverse
        gated = (normed * gates).astype(BF16)
        grad_att[...] = ((grad_rows * gates - mean_t - normed * mean_tn) * inverse).astype(BF16)
        grad_gated[i % 2] = grad_rows * normed
        local = rows_of(i % own_blocks)

        @pl.when(is_own(i))
        def _():
            gated_own[local, :] = gated

        @pl.when(jnp.logical_not(is_own(i)))
        def _():
            gated_send[local, :] = gated
            send_gated(i % own_blocks).start()

    def backward_pair(i, j):
        for number in range(heads):
            at = head(number)
            grad_rows = grad_att[:, at]
            grad_p = dot(grad_rows, value[rows_of(j), at], NT)
            twice = pair_ref(soft_slope, i, number, j)[...]
            grad_s = (grad_p * twice.astype(F32)).astype(BF16)
            grad_v[rows_of(j), at] += dot(pair_ref(soft, i, number, j)[...], grad_rows, TN)
            grad_k[rows_of(j), at] += dot(grad_s, query[rows_of(i), at], TN)
            grad_q[:, at] += dot(grad_s, keyrow[rows_of(j), at])

    def backward(i):
        combine(i)
        grad_q[...] = jnp.zeros_like(grad_q)

        for j in range(i + 1):
            backward_pair(i, j)

        here = rows_of(i)
        total = jnp.zeros((block, width), F32)
        for part in range(4):
            if part == 0:
                term = grad_gated[i % 2]
            elif part == 1:
                term = jnp.where(valid(i, block), grad_v[here, :], 0.0)
            elif part == 2:
                term = grad_q[...] * (0.5 * SCALE)
            else:
                term = grad_k[here, :] * (0.5 * SCALE)
            slopes = slope[here, part * cols : (part + 1) * cols].astype(F32)
            total = total + dot((term * slopes).astype(BF16), weights_own[part], NT)
        local = rows_of(i % own_blocks)

        @pl.when(is_own(i))
        def _():
            gx_own[local, :] = total

        @pl.when(jnp.logical_not(is_own(i)))
        def _():
            gx_send[local, :] = total.astype(BF16)
            send_gx(i % own_blocks).start()

    give = functools.partial(exchange, side, cap, send, back, back_out_sem, back_in_sem)

    def sums_back(step):
        for lane in range(side):
            base = place(step, lane, side, 1) * cap
            picked[lane * cap : (lane + 1) * cap, 0:positions] = multi_hot(
                slots, base, cap, 0, positions
            )
        row = pl.multiple_of(step * lanes, lanes)
        send[pl.ds(row, lanes), :] = dot(picked[:, 0:positions], grads[...]).astype(BF16)

    def start_give(step, first_lane):
        for lane in range(first_lane, side):
            give(step, lane).start()

    def give_all():
        for index in reversed(range(own_blocks)):
            here = rows_of(index)
            normal_x, inverse = normalize(index)
            send_gx(index).wait_recv()
            grad_x = gx_own[here, :] + gx_recv[here, :].astype(F32)
            middle = jnp.mean(grad_x, axis=-1, keepdims=True)
            along = jnp.mean(grad_x * normal_x, axis=-1, keepdims=True)
            masked = g_all[rows_of(first + index), :].astype(F32)
            grads[here, :] = (masked + (grad_x - middle - normal_x * along) * inverse).astype(BF16)
        sums_back(0)
        start_give(0, 1)
        back[0:cap, :] = send[0:cap, :]

        @pl.loop(1, steps)
        def _(step):
            sums_back(step)
            start_give(step, 0)

    forward(blocks - 1)
    for i in range(blocks - 1, -1, -1):
        if i > 0:
            forward(i - 1)
        if i == own_blocks - 1:
            pl.when(core == 1)(give_all)
        backward(i)
    pl.when(core == 0)(give_all)

    def mix(index):
        here = rows_of(index)
        send_gated(index).wait_recv()
        mixed = dot(gated_own[here, :], w_out[pl.ds(own_cols, cols), :]) + dot(
            gated_recv[here, :], w_out[pl.ds(their_cols, cols), :]
        )
        cotangent[here, :] = jnp.where(
            valid(first + index, block), embedded[here, :] + mixed, 0.0
        ).astype(BF16)

    for index in range(own_blocks):
        mix(index)
    store = pltpu.make_async_copy(cotangent, layer_out, store_sem.at[0])
    store.start()
    total = grad_k
    total[...] = jnp.zeros_like(total)

    def add(step, first_lane):
        ids = [serve[pl.ds(place(step, lane, side, -1), 1), :] for lane in range(side)]
        one_hot = jnp.where(
            jnp.concatenate(ids, axis=1) == iota((table_rows, lanes), 0), 1.0, 0.0
        ).astype(BF16)
        for lane in range(first_lane, side):
            give(step, lane).wait_recv()
        row = pl.multiple_of(step * lanes, lanes)
        total[...] += dot(one_hot, back[pl.ds(row, lanes), :])

    for_steps(side, add)
    half = table_rows // 2
    mine = pl.ds(pl.multiple_of(core * half, half), half)
    theirs = pl.ds(pl.multiple_of((1 - core) * half, half), half)
    half_send[...] = total[theirs, :].astype(BF16)
    swap = copy_over(half_send, their_half, at_half)
    swap.start()
    grads[...] = total[mine, :].astype(BF16)
    last = pltpu.make_async_copy(grads, own_half, store_sem.at[1])
    last.start()

    def given(step, first_lane):
        for lane in range(first_lane, side):
            give(step, lane).wait_send()

    for_steps(side, given)
    for index in range(own_blocks):
        send_x(index).wait_send()
        send_g(index).wait_send()
        send_gated(index).wait_send()
        send_gx(index).wait_send()

    @pl.loop(0, blocks)
    def _(i):
        send_stat(i).wait_send()

    store.wait()
    last.wait()
    swap.wait()


def finish_kernel(rows, own, their, rows_out, total_out, held, mine, theirs, sums, load_sem, store_sem):
    parts = load_sem.shape[0] // 3
    size = own.shape[0] // parts
    here = [slice(part * size, (part + 1) * size) for part in range(parts)]

    def copy(src, dst, part, sem):
        return pltpu.make_async_copy(src.at[here[part]], dst.at[here[part]], sem)

    loads = [
        [copy(src, dst, part, load_sem.at[3 * part + number])
         for number, (src, dst) in enumerate(((own, mine), (their, theirs), (rows, held)))]
        for part in range(parts)
    ]
    for load in loads:
        for each in load:
            each.start()
    stores = []
    for part in range(parts):
        for each in loads[part]:
            each.wait()
        sums[here[part], :] = mine[here[part], :].astype(F32) + theirs[here[part], :].astype(F32)
        stores.append(copy(sums, total_out, part, store_sem.at[2 * part]))
        stores.append(copy(held, rows_out, part, store_sem.at[2 * part + 1]))
        for store in stores[-2:]:
            store.start()
    for store in stores:
        store.wait()


def finish(rows, own, their):
    anywhere = pl.BlockSpec(memory_space=pl.ANY)
    assert rows.shape == own.shape
    return pl.pallas_call(
        finish_kernel,
        out_shape=(
            jax.ShapeDtypeStruct(rows.shape, rows.dtype),
            jax.ShapeDtypeStruct(own.shape, F32),
        ),
        in_specs=[anywhere] * 3,
        out_specs=(anywhere, anywhere),
        scratch_shapes=[
            pltpu.VMEM(rows.shape, rows.dtype),
            pltpu.VMEM(own.shape, own.dtype),
            pltpu.VMEM(their.shape, their.dtype),
            pltpu.VMEM(own.shape, F32),
            pltpu.SemaphoreType.DMA((12,)),
            pltpu.SemaphoreType.DMA((8,)),
        ],
        compiler_params=pltpu.CompilerParams(vmem_limit_bytes=63 << 20),
        name="finish",
    )(rows, own, their)


def on_device(side, item_table, serve_rows, token_slots, lengths, w_proj, w_out, grad_out):
    slots = token_slots[0].T
    cap = serve_rows.shape[1]
    chips = side**3
    table_rows, width = item_table.shape
    positions = slots.shape[1]
    block = min(512, positions)
    total = 2 * positions
    cols = w_out.shape[0] // 2
    heads = cols // HEAD
    own_blocks = positions // block
    blocks = 2 * own_blocks
    copies = 4 * own_blocks + blocks + 1
    anywhere = pl.BlockSpec(memory_space=pl.ANY)
    sems = pltpu.SemaphoreType.DMA

    def rows_b(rows, columns):
        return pltpu.VMEM((rows, columns), BF16)

    def rows_f(rows, columns):
        return pltpu.VMEM((rows, columns), F32)

    pairs = rows_b(2 * heads * blocks * block, block)
    scratch = {
        "serve": pltpu.VMEM(serve_rows.shape, jnp.int32),
        "slots": pltpu.VMEM(slots.shape, jnp.int32),
        "weights_own": pltpu.VMEM((4, width, cols), BF16),
        "w_out": pltpu.VMEM(w_out.shape, BF16),
        "cotangent": rows_b(positions, width),
        "picked": rows_b(side * cap, table_rows),
        "send": rows_b(chips * cap, width),
        "recv": rows_b(chips * cap, width),
        "back": rows_b(chips * cap, width),
        "turned": rows_f(width, positions),
        "embedded": rows_f(positions, width),
        "x_all": rows_b(total, width),
        "g_all": rows_b(total, width),
        "gate": rows_b(total, cols),
        "value": rows_b(total, cols),
        "query": rows_b(total, cols),
        "keyrow": rows_b(total, cols),
        "slope": rows_b(total, 4 * cols),
        "grad_gated": pltpu.VMEM((2, block, cols), F32),
        "attended": pltpu.VMEM((2, block, cols), F32),
        "stat_send": rows_f(total, 128),
        "stat_recv": rows_f(total, 128),
        "soft": pairs,
        "soft_slope": pairs,
        "grad_att": rows_b(block, cols),
        "grad_q": rows_f(block, cols),
        "grad_k": rows_f(total, cols),
        "grad_v": rows_f(total, cols),
        "gated_own": rows_b(positions, cols),
        "gated_send": rows_b(positions, cols),
        "gated_recv": rows_b(positions, cols),
        "gx_own": rows_f(positions, width),
        "gx_send": rows_b(positions, width),
        "gx_recv": rows_b(positions, width),
        "grads": rows_b(positions, width),
        "half_send": rows_b(table_rows // 2, width),
        "load_sem": sems((9,)),
        "store_sem": sems((2,)),
        "out_sem": sems((chips,)),
        "in_sem": sems((chips,)),
        "back_out_sem": sems((chips,)),
        "back_in_sem": sems((chips,)),
        "core_out_sem": sems((copies,)),
        "core_in_sem": sems((copies,)),
    }
    results = pl.pallas_call(
        functools.partial(kernel, side, cap, block),
        out_shape=(
            jax.ShapeDtypeStruct((positions, width), BF16),
            jax.ShapeDtypeStruct((table_rows // 2, width), BF16),
            jax.ShapeDtypeStruct((table_rows // 2, width), BF16),
        ),
        in_specs=[anywhere] * 3 + [pl.BlockSpec(memory_space=pltpu.SMEM)] + [anywhere] * 3,
        out_specs=(anywhere,) * 3,
        scratch_shapes=list(scratch.values()),
        compiler_params=pltpu.CompilerParams(
            collective_id=0, has_side_effects=True, vmem_limit_bytes=63 << 20
        ),
        name="hstu",
    )(item_table, serve_rows, slots, lengths, w_proj, w_out, grad_out[0])
    layer_out, grad_table = finish(*results)
    return (layer_out[None], grad_table)


def solution(mesh):
    placed = (
        P("table", None),
        P("table", "ctx"),
        P("table", "ctx", None),
        P("table"),
        P(),
        P(),
        P("table", "ctx", None),
    )
    side = round(mesh.shape["table"] ** (1 / 3))
    return jax.shard_map(
        functools.partial(on_device, side),
        mesh=mesh,
        in_specs=placed,
        out_specs=(P("table", "ctx", None), P(("table", "ctx"), None)),
        check_vma=False,
    )
```

```python
import functools

import jax
import jax.numpy as jnp
from jax import lax
from jax.experimental import pallas as pl
from jax.experimental.pallas import tpu as pltpu
from jax.sharding import PartitionSpec as P

HEAD = 128
EPS = 1e-05
SCALE = HEAD**-0.5
MESH = pl.DeviceIdType.MESH
F32 = jnp.float32
BF16 = jnp.bfloat16
NN = (((1,), (0,)), ((), ()))
NT = (((1,), (1,)), ((), ()))
TN = (((0,), (0,)), ((), ()))


def dot(a, b, form=NN):
    return lax.dot_general(a, b, form, preferred_element_type=F32)


def iota(shape, dim):
    return lax.broadcasted_iota(jnp.int32, shape, dim)


def place(step, lane, side, sign):
    me = lax.axis_index("table")
    z, y, x = lax.div(me, side * side), lax.rem(lax.div(me, side), side), lax.rem(me, side)
    far = lax.div(step, side) if isinstance(step, jax.Array) else step // side
    if sign > 0:
        z, y, x = z + lane, y + far + lane, x + step + lane
    else:
        z, y, x = z - lane + side, y - far - lane + 2 * side, x - step - lane + (side + 1) * side
    return (lax.rem(z, side) * side + lax.rem(y, side)) * side + lax.rem(x, side)


def greet_all(side):
    barrier = pltpu.get_barrier_semaphore()
    core = lax.axis_index("ctx")

    def greet(step, lane):
        pl.semaphore_signal(
            barrier, inc=1, device_id=(place(step, lane, side, 1), core), device_id_type=MESH
        )

    for lane in range(1, side):
        greet(0, lane)

    @pl.loop(1, side * side)
    def _(step):
        for lane in range(side):
            greet(step, lane)


def exchange(side, cap, send, recv, send_sem, recv_sem, step, lane):
    row = pl.multiple_of((step * side + lane) * cap, cap)
    return pltpu.make_async_remote_copy(
        src_ref=send.at[pl.ds(row, cap)],
        dst_ref=recv.at[pl.ds(row, cap)],
        send_sem=send_sem.at[step * side + lane],
        recv_sem=recv_sem.at[step * side + lane],
        device_id=(place(step, lane, side, 1), lax.axis_index("ctx")),
        device_id_type=MESH,
    )


def for_steps(side, body):
    body(0, 1)

    @pl.loop(1, side * side)
    def _(step):
        body(step, 0)


def multi_hot(slots_ref, base, rows, start, columns):
    row = iota((rows, columns), 0).astype(F32).astype(BF16)
    total = jnp.zeros((rows, columns), BF16)
    for feature in range(slots_ref.shape[0]):
        inside = slots_ref[feature : feature + 1, start : start + columns] - base
        inside = jnp.clip(inside, -1, rows).astype(F32).astype(BF16)
        total = total + jnp.where(inside == row, jnp.ones((), BF16), jnp.zeros((), BF16))
    return total


def kernel(
    side, cap, block,
    table_in, serve_in, slots_in, lengths_in, w_proj_in, w_out_in, cotangent_in,
    layer_out, own_half, their_half,
    lengths, serve, slots, weights_own, w_out, cotangent, picked, send, recv, back, turned, embedded,
    x_all, g_all, gate, value, query, keyrow, slope, grad_gated, attended, stat_send, stat_recv,
    soft, soft_slope, grad_att, grad_q, grad_k, grad_v, gated_own, gated_send, gated_recv,
    gx_own, gx_send, gx_recv, grads, half_send,
    load_sem, store_sem, out_sem, in_sem, back_out_sem, back_in_sem, core_out_sem, core_in_sem,
):
    table, core = lax.axis_index("table"), lax.axis_index("ctx")
    other = (table, 1 - core)
    barrier = pltpu.get_barrier_semaphore()
    steps = side * side
    lanes = side * cap
    table_rows, width = grad_k.shape
    positions = slots.shape[1]
    cols = value.shape[1]
    heads = cols // HEAD
    own_blocks = positions // block
    blocks = 2 * own_blocks
    first = core * own_blocks
    own_cols = pl.multiple_of(core * cols, cols)
    their_cols = pl.multiple_of((1 - core) * cols, cols)

    loads = [(serve_in, serve), (table_in, grad_k), (slots_in, slots), (cotangent_in, cotangent)]
    for part in range(4):
        here = pl.multiple_of(part * 2 * cols + core * cols, cols)
        loads.append((w_proj_in.at[:, pl.ds(here, cols)], weights_own.at[part]))
    loads.append((w_out_in, w_out))
    loads.append((lengths_in, lengths))
    loads = [
        pltpu.make_async_copy(src, dst, load_sem.at[number])
        for number, (src, dst) in enumerate(loads)
    ]
    for load in loads[:2]:
        load.start()
    greet_all(side)
    pl.semaphore_signal(barrier, inc=1, device_id=other, device_id_type=MESH)
    for load in loads[2:]:
        load.start()

    rounded = keyrow
    loads[0].wait()
    loads[1].wait()
    rounded[...] = grad_k[...].astype(BF16)
    square = iota((cap, cap), 0) == iota((cap, cap), 1)
    columns = iota((cap, table_rows), 1)

    def pick(step):
        for lane in range(side):
            ids = serve[pl.ds(place(step, lane, side, 1), 1), :]
            ids = jnp.sum(jnp.where(square, ids.astype(F32), 0.0), axis=1, keepdims=True)
            one_hot = jnp.where(ids.astype(jnp.int32) == columns, 1.0, 0.0)
            picked[lane * cap : (lane + 1) * cap, :] = one_hot.astype(BF16)
        row = pl.multiple_of(step * lanes, lanes)
        send[pl.ds(row, lanes), :] = dot(picked[...], rounded[...]).astype(BF16)

    ask = functools.partial(exchange, side, cap, send, recv, out_sem, in_sem)

    def start_ask(step, first_lane):
        for lane in range(first_lane, side):
            ask(step, lane).start()

    early = 2
    for step in range(early):
        pick(step)
    pl.semaphore_wait(barrier, side**3)
    for step in range(early):
        start_ask(step, 1 if step == 0 else 0)
    recv[0:cap, :] = send[0:cap, :]

    @pl.loop(early, steps)
    def _(step):
        pick(step)
        start_ask(step, 0)

    for load in loads[2:]:
        load.wait()
    length = lengths[0]

    def rows_of(index):
        if isinstance(index, int):
            return pl.ds(index * block, block)
        return pl.ds(pl.multiple_of(index * block, block), block)

    def valid(index, height):
        return iota((height, 1), 0) + index * block < length

    def copy_over(src, dst, number):
        return pltpu.make_async_remote_copy(
            src_ref=src,
            dst_ref=dst,
            send_sem=core_out_sem.at[number],
            recv_sem=core_in_sem.at[number],
            device_id=other,
            device_id_type=MESH,
        )

    at_g, at_x = 0, own_blocks
    at_stat = 2 * own_blocks
    at_gated = at_stat + blocks
    at_gx = at_gated + own_blocks
    at_half = at_gx + own_blocks

    def send_x(index):
        here = rows_of(first + index)
        return copy_over(x_all.at[here], x_all.at[here], at_x + index)

    def send_g(index):
        here = rows_of(first + index)
        return copy_over(g_all.at[here], g_all.at[here], at_g + index)

    for index in range(own_blocks):
        rows_g = cotangent[rows_of(index), :]
        g_all[rows_of(first + index), :] = jnp.where(
            valid(first + index, block), rows_g, jnp.zeros_like(rows_g)
        )
        send_g(index).start()
    grad_k[...] = jnp.zeros_like(grad_k)
    grad_v[...] = jnp.zeros_like(grad_v)
    turned[...] = jnp.zeros_like(turned)

    def hot_rows(index, row, count):
        return pl.ds(pl.multiple_of(index * steps * lanes + row, cap), count)

    @pl.loop(0, steps)
    def _(step):
        for lane in range(side):
            base = place(step, lane, side, -1) * cap
            row = pl.multiple_of((step * side + lane) * cap, cap)
            for index in range(own_blocks):
                soft[hot_rows(index, row, cap), :] = multi_hot(slots, base, cap, index * block, block)

    for index in range(own_blocks):
        send_g(index).wait_recv()

    def take(step, first_lane):
        for lane in range(first_lane, side):
            ask(step, lane).wait_recv()
        row = pl.multiple_of(step * lanes, lanes)
        for index in range(own_blocks):
            turned[:, index * block : (index + 1) * block] += dot(
                recv[pl.ds(row, lanes), :], soft[hot_rows(index, row, lanes), :], TN
            )

    for_steps(side, take)
    embedded[...] = turned[...].T

    def sent(step, first_lane):
        for lane in range(first_lane, side):
            ask(step, lane).wait_send()

    for_steps(side, sent)

    def normalize(index):
        rows_x = embedded[rows_of(index), :]
        centred = rows_x - jnp.mean(rows_x, axis=-1, keepdims=True)
        inverse = lax.rsqrt(jnp.mean(centred * centred, axis=-1, keepdims=True) + EPS)
        return centred * inverse, inverse

    for index in range(own_blocks):
        x_all[rows_of(first + index), :] = normalize(index)[0].astype(BF16)
        send_x(index).start()

    def project(index):
        here = rows_of(index)
        rows_x = x_all[here, :]
        for part, ref in enumerate((gate, value, query, keyrow)):
            h = dot(rows_x, weights_own[part]) * 0.5
            th = jnp.tanh(h)
            up = 1.0 + th
            act = h * up
            slope[here, part * cols : (part + 1) * cols] = (
                0.5 * (up + act * (1.0 - th))
            ).astype(BF16)
            act = act.astype(BF16)
            if part == 1:
                act = jnp.where(valid(index, block), act, jnp.zeros_like(act))
            ref[here, :] = act

    @pl.loop(0, own_blocks)
    def _(index):
        project(first + index)

    @pl.loop(0, own_blocks)
    def _(index):
        send_x(index).wait_recv()
        project((1 - core) * own_blocks + index)

    def head(number):
        return slice(number * HEAD, (number + 1) * HEAD)

    def pair_ref(ref, i, number, j):
        row = (((i % 2) * heads + number) * blocks + j) * block
        return ref.at[pl.ds(row, block)]

    def forward_pair(i, j, masked):
        for number in range(heads):
            h = dot(query[rows_of(i), head(number)], keyrow[rows_of(j), head(number)], NT)
            h = h * (0.5 * SCALE)
            th = jnp.tanh(h)
            up = 1.0 + th
            act = h * up
            twice = up + act * (1.0 - th)
            if masked:
                allowed = iota((block, block), 1) <= iota((block, block), 0)
                act = jnp.where(allowed, act, 0.0)
                twice = jnp.where(allowed, twice, 0.0)
            act = act.astype(BF16)
            pair_ref(soft, i, number, j)[...] = act
            pair_ref(soft_slope, i, number, j)[...] = twice.astype(BF16)
            added = dot(act, value[rows_of(j), head(number)])
            if masked:
                attended[i % 2, :, head(number)] = added
            else:
                attended[i % 2, :, head(number)] += added

    def send_stat(i):
        return copy_over(stat_send.at[rows_of(i)], stat_recv.at[rows_of(i)], at_stat + i)

    def forward(i):
        forward_pair(i, i, True)
        here = rows_of(i)
        grad_gated[i % 2] = dot(g_all[here, :], w_out[pl.ds(own_cols, cols), :], NT)

        for j in range(i):
            forward_pair(i, j, False)

        att = attended[i % 2]
        t = grad_gated[i % 2] * gate[here, :].astype(F32)
        lane = iota((block, 128), 1)
        sums = jnp.zeros((block, 128), F32)
        for number, term in enumerate((att, att * att, t, t * att)):
            sums = jnp.where(lane == number, jnp.sum(term, axis=1, keepdims=True), sums)
        stat_send[here, :] = sums
        send_stat(i).start()

    def is_own(i):
        return (i // own_blocks) == core

    def send_gated(index):
        here = rows_of(index)
        return copy_over(gated_send.at[here], gated_recv.at[here], at_gated + index)

    def send_gx(index):
        here = rows_of(index)
        return copy_over(gx_send.at[here], gx_recv.at[here], at_gx + index)

    def combine(i):
        here = rows_of(i)
        send_stat(i).wait_recv()
        mean = (stat_send[here, :] + stat_recv[here, :]) * (1.0 / (2 * cols))
        middle = mean[:, 0:1]
        inverse = lax.rsqrt(mean[:, 1:2] - middle * middle + EPS)
        mean_t = mean[:, 2:3]
        mean_tn = (mean[:, 3:4] - middle * mean_t) * inverse
        gates = gate[here, :].astype(F32)
        grad_rows = grad_gated[i % 2]
        normed = (attended[i % 2] - middle) * inverse
        gated = (normed * gates).astype(BF16)
        grad_att[...] = ((grad_rows * gates - mean_t - normed * mean_tn) * inverse).astype(BF16)
        grad_gated[i % 2] = grad_rows * normed
        local = rows_of(i % own_blocks)

        @pl.when(is_own(i))
        def _():
            gated_own[local, :] = gated

        @pl.when(jnp.logical_not(is_own(i)))
        def _():
            gated_send[local, :] = gated
            send_gated(i % own_blocks).start()

    def backward_pair(i, j):
        for number in range(heads):
            at = head(number)
            grad_rows = grad_att[:, at]
            grad_p = dot(grad_rows, value[rows_of(j), at], NT)
            twice = pair_ref(soft_slope, i, number, j)[...]
            grad_s = (grad_p * twice.astype(F32)).astype(BF16)
            grad_v[rows_of(j), at] += dot(pair_ref(soft, i, number, j)[...], grad_rows, TN)
            grad_k[rows_of(j), at] += dot(grad_s, query[rows_of(i), at], TN)
            grad_q[:, at] += dot(grad_s, keyrow[rows_of(j), at])

    def backward(i):
        combine(i)
        grad_q[...] = jnp.zeros_like(grad_q)

        for j in range(i + 1):
            backward_pair(i, j)

        here = rows_of(i)
        total = jnp.zeros((block, width), F32)
        for part in range(4):
            if part == 0:
                term = grad_gated[i % 2]
            elif part == 1:
                term = jnp.where(valid(i, block), grad_v[here, :], 0.0)
            elif part == 2:
                term = grad_q[...] * (0.5 * SCALE)
            else:
                term = grad_k[here, :] * (0.5 * SCALE)
            slopes = slope[here, part * cols : (part + 1) * cols].astype(F32)
            total = total + dot((term * slopes).astype(BF16), weights_own[part], NT)
        local = rows_of(i % own_blocks)

        @pl.when(is_own(i))
        def _():
            gx_own[local, :] = total

        @pl.when(jnp.logical_not(is_own(i)))
        def _():
            gx_send[local, :] = total.astype(BF16)
            send_gx(i % own_blocks).start()

    give = functools.partial(exchange, side, cap, send, back, back_out_sem, back_in_sem)

    def sums_back(step):
        for lane in range(side):
            base = place(step, lane, side, 1) * cap
            picked[lane * cap : (lane + 1) * cap, 0:positions] = multi_hot(
                slots, base, cap, 0, positions
            )
        row = pl.multiple_of(step * lanes, lanes)
        send[pl.ds(row, lanes), :] = dot(picked[:, 0:positions], grads[...]).astype(BF16)

    def start_give(step, first_lane):
        for lane in range(first_lane, side):
            give(step, lane).start()

    def give_all():
        for index in reversed(range(own_blocks)):
            here = rows_of(index)
            normal_x, inverse = normalize(index)
            send_gx(index).wait_recv()
            grad_x = gx_own[here, :] + gx_recv[here, :].astype(F32)
            middle = jnp.mean(grad_x, axis=-1, keepdims=True)
            along = jnp.mean(grad_x * normal_x, axis=-1, keepdims=True)
            masked = g_all[rows_of(first + index), :].astype(F32)
            grads[here, :] = (masked + (grad_x - middle - normal_x * along) * inverse).astype(BF16)
        sums_back(0)
        start_give(0, 1)
        back[0:cap, :] = send[0:cap, :]

        @pl.loop(1, steps)
        def _(step):
            sums_back(step)
            start_give(step, 0)

    forward(blocks - 1)
    for i in range(blocks - 1, -1, -1):
        if i > 0:
            forward(i - 1)
        if i == own_blocks - 1:
            pl.when(core == 1)(give_all)
        backward(i)
    pl.when(core == 0)(give_all)

    def mix(index):
        here = rows_of(index)
        send_gated(index).wait_recv()
        mixed = dot(gated_own[here, :], w_out[pl.ds(own_cols, cols), :]) + dot(
            gated_recv[here, :], w_out[pl.ds(their_cols, cols), :]
        )
        cotangent[here, :] = jnp.where(
            valid(first + index, block), embedded[here, :] + mixed, 0.0
        ).astype(BF16)

    for index in range(own_blocks):
        mix(index)
    store = pltpu.make_async_copy(cotangent, layer_out, store_sem.at[0])
    store.start()
    total = grad_k
    total[...] = jnp.zeros_like(total)

    def add(step, first_lane):
        both = [(step + later, lane) for later in range(2) for lane in range(side)]
        ids = [serve[pl.ds(place(*at, side, -1), 1), :] for at in both]
        one_hot = jnp.where(
            jnp.concatenate(ids, axis=1) == iota((table_rows, 2 * lanes), 0), 1.0, 0.0
        ).astype(BF16)
        for at in both[first_lane:]:
            give(*at).wait_recv()
        row = pl.multiple_of(step * lanes, 2 * lanes)
        total[...] += dot(one_hot, back[pl.ds(row, 2 * lanes), :])

    add(0, 1)

    @pl.loop(1, steps // 2)
    def _(pair):
        add(2 * pair, 0)

    half = table_rows // 2
    mine = pl.ds(pl.multiple_of(core * half, half), half)
    theirs = pl.ds(pl.multiple_of((1 - core) * half, half), half)
    half_send[...] = total[theirs, :].astype(BF16)
    swap = copy_over(half_send, their_half, at_half)
    swap.start()
    grads[...] = total[mine, :].astype(BF16)
    last = pltpu.make_async_copy(grads, own_half, store_sem.at[1])
    last.start()

    def given(step, first_lane):
        for lane in range(first_lane, side):
            give(step, lane).wait_send()

    for_steps(side, given)
    for index in range(own_blocks):
        send_x(index).wait_send()
        send_g(index).wait_send()
        send_gated(index).wait_send()
        send_gx(index).wait_send()

    @pl.loop(0, blocks)
    def _(i):
        send_stat(i).wait_send()

    store.wait()
    last.wait()
    swap.wait()


def finish_kernel(rows, own, their, rows_out, total_out, held, mine, theirs, sums, load_sem, store_sem):
    parts = load_sem.shape[0] // 3
    size = own.shape[0] // parts
    here = [slice(part * size, (part + 1) * size) for part in range(parts)]

    def copy(src, dst, part, sem):
        return pltpu.make_async_copy(src.at[here[part]], dst.at[here[part]], sem)

    loads = [
        [copy(src, dst, part, load_sem.at[3 * part + number])
         for number, (src, dst) in enumerate(((own, mine), (their, theirs), (rows, held)))]
        for part in range(parts)
    ]
    for load in loads:
        for each in load:
            each.start()
    stores = []
    for part in range(parts):
        for each in loads[part]:
            each.wait()
        sums[here[part], :] = mine[here[part], :].astype(F32) + theirs[here[part], :].astype(F32)
        stores.append(copy(sums, total_out, part, store_sem.at[2 * part]))
        stores.append(copy(held, rows_out, part, store_sem.at[2 * part + 1]))
        for store in stores[-2:]:
            store.start()
    for store in stores:
        store.wait()


def finish(rows, own, their):
    anywhere = pl.BlockSpec(memory_space=pl.ANY)
    assert rows.shape == own.shape
    return pl.pallas_call(
        finish_kernel,
        out_shape=(
            jax.ShapeDtypeStruct(rows.shape, rows.dtype),
            jax.ShapeDtypeStruct(own.shape, F32),
        ),
        in_specs=[anywhere] * 3,
        out_specs=(anywhere, anywhere),
        scratch_shapes=[
            pltpu.VMEM(rows.shape, rows.dtype),
            pltpu.VMEM(own.shape, own.dtype),
            pltpu.VMEM(their.shape, their.dtype),
            pltpu.VMEM(own.shape, F32),
            pltpu.SemaphoreType.DMA((12,)),
            pltpu.SemaphoreType.DMA((8,)),
        ],
        compiler_params=pltpu.CompilerParams(vmem_limit_bytes=63 << 20),
        name="finish",
    )(rows, own, their)


def on_device(side, item_table, serve_rows, token_slots, lengths, w_proj, w_out, grad_out):
    slots = token_slots[0].T
    cap = serve_rows.shape[1]
    chips = side**3
    table_rows, width = item_table.shape
    positions = slots.shape[1]
    block = min(512, positions)
    total = 2 * positions
    cols = w_out.shape[0] // 2
    heads = cols // HEAD
    own_blocks = positions // block
    blocks = 2 * own_blocks
    copies = 4 * own_blocks + blocks + 1
    anywhere = pl.BlockSpec(memory_space=pl.ANY)
    sems = pltpu.SemaphoreType.DMA

    def rows_b(rows, columns):
        return pltpu.VMEM((rows, columns), BF16)

    def rows_f(rows, columns):
        return pltpu.VMEM((rows, columns), F32)

    pairs = rows_b(2 * heads * blocks * block, block)
    scratch = {
        "lengths": pltpu.SMEM(lengths.shape, jnp.int32),
        "serve": pltpu.VMEM(serve_rows.shape, jnp.int32),
        "slots": pltpu.VMEM(slots.shape, jnp.int32),
        "weights_own": pltpu.VMEM((4, width, cols), BF16),
        "w_out": pltpu.VMEM(w_out.shape, BF16),
        "cotangent": rows_b(positions, width),
        "picked": rows_b(side * cap, table_rows),
        "send": rows_b(chips * cap, width),
        "recv": rows_b(chips * cap, width),
        "back": rows_b(chips * cap, width),
        "turned": rows_f(width, positions),
        "embedded": rows_f(positions, width),
        "x_all": rows_b(total, width),
        "g_all": rows_b(total, width),
        "gate": rows_b(total, cols),
        "value": rows_b(total, cols),
        "query": rows_b(total, cols),
        "keyrow": rows_b(total, cols),
        "slope": rows_b(total, 4 * cols),
        "grad_gated": pltpu.VMEM((2, block, cols), F32),
        "attended": pltpu.VMEM((2, block, cols), F32),
        "stat_send": rows_f(total, 128),
        "stat_recv": rows_f(total, 128),
        "soft": pairs,
        "soft_slope": pairs,
        "grad_att": rows_b(block, cols),
        "grad_q": rows_f(block, cols),
        "grad_k": rows_f(total, cols),
        "grad_v": rows_f(total, cols),
        "gated_own": rows_b(positions, cols),
        "gated_send": rows_b(positions, cols),
        "gated_recv": rows_b(positions, cols),
        "gx_own": rows_f(positions, width),
        "gx_send": rows_b(positions, width),
        "gx_recv": rows_b(positions, width),
        "grads": rows_b(positions, width),
        "half_send": rows_b(table_rows // 2, width),
        "load_sem": sems((10,)),
        "store_sem": sems((2,)),
        "out_sem": sems((chips,)),
        "in_sem": sems((chips,)),
        "back_out_sem": sems((chips,)),
        "back_in_sem": sems((chips,)),
        "core_out_sem": sems((copies,)),
        "core_in_sem": sems((copies,)),
    }
    results = pl.pallas_call(
        functools.partial(kernel, side, cap, block),
        out_shape=(
            jax.ShapeDtypeStruct((positions, width), BF16),
            jax.ShapeDtypeStruct((table_rows // 2, width), BF16),
            jax.ShapeDtypeStruct((table_rows // 2, width), BF16),
        ),
        in_specs=[anywhere] * 7,
        out_specs=(anywhere,) * 3,
        scratch_shapes=list(scratch.values()),
        compiler_params=pltpu.CompilerParams(
            collective_id=0, has_side_effects=True, vmem_limit_bytes=63 << 20
        ),
        name="hstu",
    )(item_table, serve_rows, slots, lengths, w_proj, w_out, grad_out[0])
    layer_out, grad_table = finish(*results)
    return (layer_out[None], grad_table)


def solution(mesh):
    placed = (
        P("table", None),
        P("table", "ctx"),
        P("table", "ctx", None),
        P("table"),
        P(),
        P(),
        P("table", "ctx", None),
    )
    side = round(mesh.shape["table"] ** (1 / 3))
    return jax.shard_map(
        functools.partial(on_device, side),
        mesh=mesh,
        in_specs=placed,
        out_specs=(P("table", "ctx", None), P(("table", "ctx"), None)),
        check_vma=False,
    )
```

```python
import functools

import jax
import jax.numpy as jnp
from jax import lax
from jax.experimental import pallas as pl
from jax.experimental.pallas import tpu as pltpu
from jax.sharding import PartitionSpec as P

HEAD = 128
EPS = 1e-05
SCALE = HEAD**-0.5
MESH = pl.DeviceIdType.MESH
F32 = jnp.float32
BF16 = jnp.bfloat16
NN = (((1,), (0,)), ((), ()))
NT = (((1,), (1,)), ((), ()))
TN = (((0,), (0,)), ((), ()))


def dot(a, b, form=NN):
    return lax.dot_general(a, b, form, preferred_element_type=F32)


def iota(shape, dim):
    return lax.broadcasted_iota(jnp.int32, shape, dim)


def place(step, lane, side, sign):
    me = lax.axis_index("table")
    z, y, x = lax.div(me, side * side), lax.rem(lax.div(me, side), side), lax.rem(me, side)
    far = lax.div(step, side) if isinstance(step, jax.Array) else step // side
    if sign > 0:
        z, y, x = z + lane, y + far + lane, x + step + lane
    else:
        z, y, x = z - lane + side, y - far - lane + 2 * side, x - step - lane + (side + 1) * side
    return (lax.rem(z, side) * side + lax.rem(y, side)) * side + lax.rem(x, side)


def greet_all(side):
    barrier = pltpu.get_barrier_semaphore()
    core = lax.axis_index("ctx")

    def greet(step, lane):
        pl.semaphore_signal(
            barrier, inc=1, device_id=(place(step, lane, side, 1), core), device_id_type=MESH
        )

    for lane in range(1, side):
        greet(0, lane)

    @pl.loop(1, side * side)
    def _(step):
        for lane in range(side):
            greet(step, lane)


def exchange(side, cap, send, recv, send_sem, recv_sem, step, lane):
    row = pl.multiple_of((step * side + lane) * cap, cap)
    return pltpu.make_async_remote_copy(
        src_ref=send.at[pl.ds(row, cap)],
        dst_ref=recv.at[pl.ds(row, cap)],
        send_sem=send_sem.at[step * side + lane],
        recv_sem=recv_sem.at[step * side + lane],
        device_id=(place(step, lane, side, 1), lax.axis_index("ctx")),
        device_id_type=MESH,
    )


def for_steps(side, body):
    body(0, 1)

    @pl.loop(1, side * side)
    def _(step):
        body(step, 0)


def multi_hot(slots_ref, base, rows, start, columns):
    row = iota((rows, columns), 0).astype(F32).astype(BF16)
    total = jnp.zeros((rows, columns), BF16)
    for feature in range(slots_ref.shape[0]):
        inside = slots_ref[feature : feature + 1, start : start + columns] - base
        inside = jnp.clip(inside, -1, rows).astype(F32).astype(BF16)
        total = total + jnp.where(inside == row, jnp.ones((), BF16), jnp.zeros((), BF16))
    return total


def kernel(
    side, cap, block,
    table_in, serve_in, slots_in, lengths_in, w_proj_in, w_out_in, cotangent_in,
    layer_out, own_half, their_half,
    lengths, serve, slots, weights_own, w_out, cotangent, picked, send, recv, back, turned, embedded,
    x_all, g_all, gate, value, query, keyrow, slope, grad_gated, attended, stat_send, stat_recv,
    soft, soft_slope, grad_att, grad_q, grad_k, grad_v, gated_own, gated_send, gated_recv,
    gx_own, gx_send, gx_recv, grads, half_send,
    load_sem, store_sem, out_sem, in_sem, back_out_sem, back_in_sem, core_out_sem, core_in_sem,
):
    table, core = lax.axis_index("table"), lax.axis_index("ctx")
    other = (table, 1 - core)
    barrier = pltpu.get_barrier_semaphore()
    steps = side * side
    lanes = side * cap
    table_rows, width = grad_k.shape
    positions = slots.shape[1]
    cols = value.shape[1]
    heads = cols // HEAD
    own_blocks = positions // block
    blocks = 2 * own_blocks
    first = core * own_blocks
    own_cols = pl.multiple_of(core * cols, cols)
    their_cols = pl.multiple_of((1 - core) * cols, cols)

    loads = [(serve_in, serve), (table_in, grad_k), (slots_in, slots), (cotangent_in, cotangent)]
    for part in range(4):
        here = pl.multiple_of(part * 2 * cols + core * cols, cols)
        loads.append((w_proj_in.at[:, pl.ds(here, cols)], weights_own.at[part]))
    loads.append((w_out_in, w_out))
    loads.append((lengths_in, lengths))
    loads = [
        pltpu.make_async_copy(src, dst, load_sem.at[number])
        for number, (src, dst) in enumerate(loads)
    ]
    for load in loads[:2]:
        load.start()
    greet_all(side)
    pl.semaphore_signal(barrier, inc=1, device_id=other, device_id_type=MESH)
    for load in loads[2:]:
        load.start()

    rounded = keyrow
    loads[0].wait()
    loads[1].wait()
    rounded[...] = grad_k[...].astype(BF16)
    square = iota((cap, cap), 0) == iota((cap, cap), 1)
    columns = iota((cap, table_rows), 1)

    def pick(step):
        for lane in range(side):
            ids = serve[pl.ds(place(step, lane, side, 1), 1), :]
            ids = jnp.sum(jnp.where(square, ids.astype(F32), 0.0), axis=1, keepdims=True)
            one_hot = jnp.where(ids.astype(jnp.int32) == columns, 1.0, 0.0)
            picked[lane * cap : (lane + 1) * cap, :] = one_hot.astype(BF16)
        row = pl.multiple_of(step * lanes, lanes)
        send[pl.ds(row, lanes), :] = dot(picked[...], rounded[...]).astype(BF16)

    ask = functools.partial(exchange, side, cap, send, recv, out_sem, in_sem)

    def start_ask(step, first_lane):
        for lane in range(first_lane, side):
            ask(step, lane).start()

    early = 2
    for step in range(early):
        pick(step)
    pl.semaphore_wait(barrier, side**3)
    for step in range(early):
        start_ask(step, 1 if step == 0 else 0)
    recv[0:cap, :] = send[0:cap, :]

    @pl.loop(early, steps)
    def _(step):
        pick(step)
        start_ask(step, 0)

    for load in loads[2:]:
        load.wait()
    length = lengths[0]

    def rows_of(index):
        if isinstance(index, int):
            return pl.ds(index * block, block)
        return pl.ds(pl.multiple_of(index * block, block), block)

    def valid(index, height):
        return iota((height, 1), 0) + index * block < length

    def copy_over(src, dst, number):
        return pltpu.make_async_remote_copy(
            src_ref=src,
            dst_ref=dst,
            send_sem=core_out_sem.at[number],
            recv_sem=core_in_sem.at[number],
            device_id=other,
            device_id_type=MESH,
        )

    at_g, at_x = 0, own_blocks
    at_stat = 2 * own_blocks
    at_gated = at_stat + blocks
    at_gx = at_gated + own_blocks
    at_half = at_gx + own_blocks

    def send_x(index):
        here = rows_of(first + index)
        return copy_over(x_all.at[here], x_all.at[here], at_x + index)

    def send_g(index):
        here = rows_of(first + index)
        return copy_over(g_all.at[here], g_all.at[here], at_g + index)

    for index in range(own_blocks):
        rows_g = cotangent[rows_of(index), :]
        g_all[rows_of(first + index), :] = jnp.where(
            valid(first + index, block), rows_g, jnp.zeros_like(rows_g)
        )
        send_g(index).start()
    grad_k[...] = jnp.zeros_like(grad_k)
    grad_v[...] = jnp.zeros_like(grad_v)
    turned[...] = jnp.zeros_like(turned)

    def hot_rows(index, row, count):
        return pl.ds(pl.multiple_of(index * steps * lanes + row, cap), count)

    @pl.loop(0, steps)
    def _(step):
        for lane in range(side):
            base = place(step, lane, side, -1) * cap
            row = pl.multiple_of((step * side + lane) * cap, cap)
            for index in range(own_blocks):
                soft[hot_rows(index, row, cap), :] = multi_hot(slots, base, cap, index * block, block)

    for index in range(own_blocks):
        send_g(index).wait_recv()

    def take(step, first_lane):
        for lane in range(first_lane, side):
            ask(step, lane).wait_recv()
        row = pl.multiple_of(step * lanes, lanes)
        for index in range(own_blocks):
            turned[:, index * block : (index + 1) * block] += dot(
                recv[pl.ds(row, lanes), :], soft[hot_rows(index, row, lanes), :], TN
            )

    for_steps(side, take)
    embedded[...] = turned[...].T

    def normalize(index):
        rows_x = embedded[rows_of(index), :]
        centred = rows_x - jnp.mean(rows_x, axis=-1, keepdims=True)
        inverse = lax.rsqrt(jnp.mean(centred * centred, axis=-1, keepdims=True) + EPS)
        return centred * inverse, inverse

    for index in range(own_blocks):
        x_all[rows_of(first + index), :] = normalize(index)[0].astype(BF16)
        send_x(index).start()

    def project(index):
        here = rows_of(index)
        rows_x = x_all[here, :]
        for part, ref in enumerate((gate, value, query, keyrow)):
            h = dot(rows_x, weights_own[part]) * 0.5
            th = jnp.tanh(h)
            up = 1.0 + th
            act = h * up
            slope[here, part * cols : (part + 1) * cols] = (
                0.5 * (up + act * (1.0 - th))
            ).astype(BF16)
            act = act.astype(BF16)
            if part == 1:
                act = jnp.where(valid(index, block), act, jnp.zeros_like(act))
            ref[here, :] = act

    @pl.loop(0, own_blocks)
    def _(index):
        project(first + index)

    @pl.loop(0, own_blocks)
    def _(index):
        send_x(index).wait_recv()
        project((1 - core) * own_blocks + index)

    def head(number):
        return slice(number * HEAD, (number + 1) * HEAD)

    def pair_ref(ref, i, number, j):
        row = (((i % 2) * heads + number) * blocks + j) * block
        return ref.at[pl.ds(row, block)]

    def forward_pair(i, j, masked):
        for number in range(heads):
            h = dot(query[rows_of(i), head(number)], keyrow[rows_of(j), head(number)], NT)
            h = h * (0.5 * SCALE)
            th = jnp.tanh(h)
            up = 1.0 + th
            act = h * up
            twice = up + act * (1.0 - th)
            if masked:
                allowed = iota((block, block), 1) <= iota((block, block), 0)
                act = jnp.where(allowed, act, 0.0)
                twice = jnp.where(allowed, twice, 0.0)
            act = act.astype(BF16)
            pair_ref(soft, i, number, j)[...] = act
            pair_ref(soft_slope, i, number, j)[...] = twice.astype(BF16)
            added = dot(act, value[rows_of(j), head(number)])
            if masked:
                attended[i % 2, :, head(number)] = added
            else:
                attended[i % 2, :, head(number)] += added

    def send_stat(i):
        return copy_over(stat_send.at[rows_of(i)], stat_recv.at[rows_of(i)], at_stat + i)

    def forward(i):
        forward_pair(i, i, True)
        here = rows_of(i)
        grad_gated[i % 2] = dot(g_all[here, :], w_out[pl.ds(own_cols, cols), :], NT)

        for j in range(i):
            forward_pair(i, j, False)

        att = attended[i % 2]
        t = grad_gated[i % 2] * gate[here, :].astype(F32)
        lane = iota((block, 128), 1)
        sums = jnp.zeros((block, 128), F32)
        for number, term in enumerate((att, att * att, t, t * att)):
            sums = jnp.where(lane == number, jnp.sum(term, axis=1, keepdims=True), sums)
        stat_send[here, :] = sums
        send_stat(i).start()

    def is_own(i):
        return (i // own_blocks) == core

    def send_gated(index):
        here = rows_of(index)
        return copy_over(gated_send.at[here], gated_recv.at[here], at_gated + index)

    def send_gx(index):
        here = rows_of(index)
        return copy_over(gx_send.at[here], gx_recv.at[here], at_gx + index)

    def combine(i):
        here = rows_of(i)
        send_stat(i).wait_recv()
        mean = (stat_send[here, :] + stat_recv[here, :]) * (1.0 / (2 * cols))
        middle = mean[:, 0:1]
        inverse = lax.rsqrt(mean[:, 1:2] - middle * middle + EPS)
        mean_t = mean[:, 2:3]
        mean_tn = (mean[:, 3:4] - middle * mean_t) * inverse
        gates = gate[here, :].astype(F32)
        grad_rows = grad_gated[i % 2]
        normed = (attended[i % 2] - middle) * inverse
        gated = (normed * gates).astype(BF16)
        grad_att[...] = ((grad_rows * gates - mean_t - normed * mean_tn) * inverse).astype(BF16)
        grad_gated[i % 2] = grad_rows * normed
        local = rows_of(i % own_blocks)

        @pl.when(is_own(i))
        def _():
            gated_own[local, :] = gated

        @pl.when(jnp.logical_not(is_own(i)))
        def _():
            gated_send[local, :] = gated
            send_gated(i % own_blocks).start()

    def backward_pair(i, j):
        for number in range(heads):
            at = head(number)
            grad_rows = grad_att[:, at]
            grad_p = dot(grad_rows, value[rows_of(j), at], NT)
            twice = pair_ref(soft_slope, i, number, j)[...]
            grad_s = (grad_p * twice.astype(F32)).astype(BF16)
            grad_v[rows_of(j), at] += dot(pair_ref(soft, i, number, j)[...], grad_rows, TN)
            grad_k[rows_of(j), at] += dot(grad_s, query[rows_of(i), at], TN)
            grad_q[:, at] += dot(grad_s, keyrow[rows_of(j), at])

    def backward(i):
        combine(i)
        grad_q[...] = jnp.zeros_like(grad_q)

        for j in range(i + 1):
            backward_pair(i, j)

        here = rows_of(i)
        total = jnp.zeros((block, width), F32)
        for part in range(4):
            if part == 0:
                term = grad_gated[i % 2]
            elif part == 1:
                term = jnp.where(valid(i, block), grad_v[here, :], 0.0)
            elif part == 2:
                term = grad_q[...] * (0.5 * SCALE)
            else:
                term = grad_k[here, :] * (0.5 * SCALE)
            slopes = slope[here, part * cols : (part + 1) * cols].astype(F32)
            total = total + dot((term * slopes).astype(BF16), weights_own[part], NT)
        local = rows_of(i % own_blocks)

        @pl.when(is_own(i))
        def _():
            gx_own[local, :] = total

        @pl.when(jnp.logical_not(is_own(i)))
        def _():
            gx_send[local, :] = total.astype(BF16)
            send_gx(i % own_blocks).start()

    forward(blocks - 1)

    for step in range(blocks - 1):
        forward(blocks - 2 - step)
        backward(blocks - 1 - step)

    backward(0)

    def mix(index):
        here = rows_of(index)
        send_gated(index).wait_recv()
        mixed = dot(gated_own[here, :], w_out[pl.ds(own_cols, cols), :]) + dot(
            gated_recv[here, :], w_out[pl.ds(their_cols, cols), :]
        )
        cotangent[here, :] = jnp.where(
            valid(first + index, block), embedded[here, :] + mixed, 0.0
        ).astype(BF16)

    for index in reversed(range(own_blocks)):
        here = rows_of(index)
        normal_x, inverse = normalize(index)
        send_gx(index).wait_recv()
        grad_x = gx_own[here, :] + gx_recv[here, :].astype(F32)
        middle = jnp.mean(grad_x, axis=-1, keepdims=True)
        along = jnp.mean(grad_x * normal_x, axis=-1, keepdims=True)
        masked = g_all[rows_of(first + index), :].astype(F32)
        grads[here, :] = (masked + (grad_x - middle - normal_x * along) * inverse).astype(BF16)

    def sent(step, first_lane):
        for lane in range(first_lane, side):
            ask(step, lane).wait_send()

    for_steps(side, sent)
    give = functools.partial(exchange, side, cap, send, back, back_out_sem, back_in_sem)

    def sums_back(step):
        for lane in range(side):
            base = place(step, lane, side, 1) * cap
            picked[lane * cap : (lane + 1) * cap, 0:positions] = multi_hot(
                slots, base, cap, 0, positions
            )
        row = pl.multiple_of(step * lanes, lanes)
        send[pl.ds(row, lanes), :] = dot(picked[:, 0:positions], grads[...]).astype(BF16)

    def start_give(step, first_lane):
        for lane in range(first_lane, side):
            give(step, lane).start()

    sums_back(0)
    start_give(0, 1)
    back[0:cap, :] = send[0:cap, :]

    @pl.loop(1, steps)
    def _(step):
        sums_back(step)
        start_give(step, 0)

    for index in range(own_blocks):
        mix(index)
    store = pltpu.make_async_copy(cotangent, layer_out, store_sem.at[0])
    store.start()
    total = grad_k
    total[...] = jnp.zeros_like(total)

    def add(step, first_lane):
        both = [(step + later, lane) for later in range(2) for lane in range(side)]
        ids = [serve[pl.ds(place(*at, side, -1), 1), :] for at in both]
        one_hot = jnp.where(
            jnp.concatenate(ids, axis=1) == iota((table_rows, 2 * lanes), 0), 1.0, 0.0
        ).astype(BF16)
        for at in both[first_lane:]:
            give(*at).wait_recv()
        row = pl.multiple_of(step * lanes, 2 * lanes)
        total[...] += dot(one_hot, back[pl.ds(row, 2 * lanes), :])

    add(0, 1)

    @pl.loop(1, steps // 2)
    def _(pair):
        add(2 * pair, 0)

    half = table_rows // 2
    mine = pl.ds(pl.multiple_of(core * half, half), half)
    theirs = pl.ds(pl.multiple_of((1 - core) * half, half), half)
    half_send[...] = total[theirs, :].astype(BF16)
    swap = copy_over(half_send, their_half, at_half)
    swap.start()
    last = pltpu.make_async_copy(total.at[mine], own_half, store_sem.at[1])
    last.start()

    def given(step, first_lane):
        for lane in range(first_lane, side):
            give(step, lane).wait_send()

    for_steps(side, given)
    for index in range(own_blocks):
        send_x(index).wait_send()
        send_g(index).wait_send()
        send_gated(index).wait_send()
        send_gx(index).wait_send()

    @pl.loop(0, blocks)
    def _(i):
        send_stat(i).wait_send()

    store.wait()
    last.wait()
    swap.wait()


def finish_kernel(rows, own, their, rows_out, total_out, held, mine, theirs, load_sem, store_sem):
    half = own.shape[0] // 2
    loads = []
    for part in range(2):
        here = slice(part * half, (part + 1) * half)
        for number, (src, dst) in enumerate(((own, mine), (their, theirs))):
            loads.append(
                pltpu.make_async_copy(src.at[here], dst.at[here], load_sem.at[2 * part + number])
            )
    loads.append(pltpu.make_async_copy(rows, held, load_sem.at[4]))
    for load in loads:
        load.start()
    stores = []
    for part in range(2):
        here = slice(part * half, (part + 1) * half)
        loads[2 * part].wait()
        loads[2 * part + 1].wait()
        mine[here, :] = mine[here, :] + theirs[here, :].astype(F32)
        stores.append(pltpu.make_async_copy(mine.at[here], total_out.at[here], store_sem.at[part]))
        stores[-1].start()
    loads[4].wait()
    stores.append(pltpu.make_async_copy(held, rows_out, store_sem.at[2]))
    stores[-1].start()
    for store in stores:
        store.wait()


def finish(rows, own, their):
    anywhere = pl.BlockSpec(memory_space=pl.ANY)
    return pl.pallas_call(
        finish_kernel,
        out_shape=(
            jax.ShapeDtypeStruct(rows.shape, rows.dtype),
            jax.ShapeDtypeStruct(own.shape, own.dtype),
        ),
        in_specs=[anywhere] * 3,
        out_specs=(anywhere, anywhere),
        scratch_shapes=[
            pltpu.VMEM(rows.shape, rows.dtype),
            pltpu.VMEM(own.shape, own.dtype),
            pltpu.VMEM(their.shape, their.dtype),
            pltpu.SemaphoreType.DMA((5,)),
            pltpu.SemaphoreType.DMA((3,)),
        ],
        compiler_params=pltpu.CompilerParams(vmem_limit_bytes=63 << 20),
        name="finish",
    )(rows, own, their)


def on_device(side, item_table, serve_rows, token_slots, lengths, w_proj, w_out, grad_out):
    slots = token_slots[0].T
    cap = serve_rows.shape[1]
    chips = side**3
    table_rows, width = item_table.shape
    positions = slots.shape[1]
    block = min(512, positions)
    total = 2 * positions
    cols = w_out.shape[0] // 2
    heads = cols // HEAD
    own_blocks = positions // block
    blocks = 2 * own_blocks
    copies = 4 * own_blocks + blocks + 1
    anywhere = pl.BlockSpec(memory_space=pl.ANY)
    sems = pltpu.SemaphoreType.DMA

    def rows_b(rows, columns):
        return pltpu.VMEM((rows, columns), BF16)

    def rows_f(rows, columns):
        return pltpu.VMEM((rows, columns), F32)

    pairs = rows_b(2 * heads * blocks * block, block)
    scratch = {
        "lengths": pltpu.SMEM(lengths.shape, jnp.int32),
        "serve": pltpu.VMEM(serve_rows.shape, jnp.int32),
        "slots": pltpu.VMEM(slots.shape, jnp.int32),
        "weights_own": pltpu.VMEM((4, width, cols), BF16),
        "w_out": pltpu.VMEM(w_out.shape, BF16),
        "cotangent": rows_b(positions, width),
        "picked": rows_b(side * cap, table_rows),
        "send": rows_b(chips * cap, width),
        "recv": rows_b(chips * cap, width),
        "back": rows_b(chips * cap, width),
        "turned": rows_f(width, positions),
        "embedded": rows_f(positions, width),
        "x_all": rows_b(total, width),
        "g_all": rows_b(total, width),
        "gate": rows_b(total, cols),
        "value": rows_b(total, cols),
        "query": rows_b(total, cols),
        "keyrow": rows_b(total, cols),
        "slope": rows_b(total, 4 * cols),
        "grad_gated": pltpu.VMEM((2, block, cols), F32),
        "attended": pltpu.VMEM((2, block, cols), F32),
        "stat_send": rows_f(total, 128),
        "stat_recv": rows_f(total, 128),
        "soft": pairs,
        "soft_slope": pairs,
        "grad_att": rows_b(block, cols),
        "grad_q": rows_f(block, cols),
        "grad_k": rows_f(total, cols),
        "grad_v": rows_f(total, cols),
        "gated_own": rows_b(positions, cols),
        "gated_send": rows_b(positions, cols),
        "gated_recv": rows_b(positions, cols),
        "gx_own": rows_f(positions, width),
        "gx_send": rows_b(positions, width),
        "gx_recv": rows_b(positions, width),
        "grads": rows_b(positions, width),
        "half_send": rows_b(table_rows // 2, width),
        "load_sem": sems((10,)),
        "store_sem": sems((2,)),
        "out_sem": sems((chips,)),
        "in_sem": sems((chips,)),
        "back_out_sem": sems((chips,)),
        "back_in_sem": sems((chips,)),
        "core_out_sem": sems((copies,)),
        "core_in_sem": sems((copies,)),
    }
    results = pl.pallas_call(
        functools.partial(kernel, side, cap, block),
        out_shape=(
            jax.ShapeDtypeStruct((positions, width), BF16),
            jax.ShapeDtypeStruct((table_rows // 2, width), F32),
            jax.ShapeDtypeStruct((table_rows // 2, width), BF16),
        ),
        in_specs=[anywhere] * 7,
        out_specs=(anywhere,) * 3,
        scratch_shapes=list(scratch.values()),
        compiler_params=pltpu.CompilerParams(
            collective_id=0, has_side_effects=True, vmem_limit_bytes=63 << 20
        ),
        name="hstu",
    )(item_table, serve_rows, slots, lengths, w_proj, w_out, grad_out[0])
    layer_out, grad_table = finish(*results)
    return (layer_out[None], grad_table)


def solution(mesh):
    placed = (
        P("table", None),
        P("table", "ctx"),
        P("table", "ctx", None),
        P("table"),
        P(),
        P(),
        P("table", "ctx", None),
    )
    side = round(mesh.shape["table"] ** (1 / 3))
    return jax.shard_map(
        functools.partial(on_device, side),
        mesh=mesh,
        in_specs=placed,
        out_specs=(P("table", "ctx", None), P(("table", "ctx"), None)),
        check_vma=False,
    )
```
